32 devices in a mesh: ctx: 4 (over z), fsdp: 8 (over y, x, core).
Axes of the slice: x: 2, y: 2, z: 4, core: 2. Of those that a mesh axis runs over, the one named last changes fastest.
Arguments:
- tokens: bfloat16 [8, 1024, 2048], P('fsdp', 'ctx'), may hold values from -6 to 6
- segments: int32 [8, 1024], P('fsdp'), may hold values from 0 to 1, as said below
- query_weight: bfloat16 [2048, 2048], P('fsdp'), may hold values from -0.125 to 0.125
- pair_weight: bfloat16 [2048, 256], P('fsdp'), may hold values from -0.125 to 0.125
- out_weight: bfloat16 [2048, 2048], P('fsdp'), may hold values from -2 to 2
- query_bias: bfloat16 [2048], P('fsdp'), may hold values from -1.5 to 1.5
- value_bias: bfloat16 [128], P('fsdp'), may hold values from -1.5 to 1.5
- out_bias: bfloat16 [2048], P('fsdp'), may hold values from -1.5 to 1.5
- norm1_gain: bfloat16 [2048], P('fsdp'), may hold values from 0.25 to 1.75
- norm1_bias: bfloat16 [2048], P('fsdp'), may hold values from -1.5 to 1.5
- fc_weight: bfloat16 [2048, 8192], P('fsdp'), may hold values from -0.125 to 0.125
- proj_weight: bfloat16 [8192, 2048], P('fsdp'), may hold values from -0.125 to 0.125
- fc_bias: bfloat16 [8192], P('fsdp'), may hold values from -1.5 to 1.5
- proj_bias: bfloat16 [2048], P('fsdp'), may hold values from -1.5 to 1.5
- norm2_gain: bfloat16 [2048], P('fsdp'), may hold values from 0.25 to 1.75
- norm2_bias: bfloat16 [2048], P('fsdp'), may hold values from -1.5 to 1.5
- cotangent: bfloat16 [8, 1024, 2048], P('fsdp', 'ctx'), may hold values from -6 to 6
Outputs:
- output: bfloat16 [8, 1024, 2048], P('fsdp', 'ctx')
- grad_tokens: bfloat16 [8, 1024, 2048], P('fsdp', 'ctx')
- grad_query_weight: float32 [2048, 2048], P('fsdp')
- grad_pair_weight: float32 [2048, 256], P('fsdp')
- grad_out_weight: float32 [2048, 2048], P('fsdp')
- grad_query_bias: float32 [2048], P('fsdp')
- grad_value_bias: float32 [128], P('fsdp')
- grad_out_bias: float32 [2048], P('fsdp')
- grad_norm1_gain: float32 [2048], P('fsdp')
- grad_norm1_bias: float32 [2048], P('fsdp')
- grad_fc_weight: float32 [2048, 8192], P('fsdp')
- grad_proj_weight: float32 [8192, 2048], P('fsdp')
- grad_fc_bias: float32 [8192], P('fsdp')
- grad_proj_bias: float32 [2048], P('fsdp')
- grad_norm2_gain: float32 [2048], P('fsdp')
- grad_norm2_bias: float32 [2048], P('fsdp')
The draws below stay inside these ranges and needn't reach their ends.
Inputs may be any that keep to these rules, and one draw needn't show every extreme that they name: `segments`: each row holds two documents numbered 0 and 1 in order of position; the first or the last of them has 1 to 255 tokens, which one is drawn per row.
All inputs are finite; a program needn't handle non-finite values.
Results may differ from the reference program's by a relative error of at most 0.019.
Values may be sent and summed in bfloat16 or wider, within the bound.
No kernel may reach another device: no remote copies, remote signals or barrier semaphores. Data moves between devices by JAX's collectives and lax.ppermute only.
A program may use at most 512 MiB of HBM per device.

```python
import math
import jax
import jax.numpy as jnp
from jax import lax

D = 2048
H = 16
HD = 128
FF = 8192
WINDOW = 1024
TOK_DEV = 256
GROUP = 1024
SEQS = 8


def draw_segments(key, part):
    key = jax.random.fold_in(key, 11)
    length_key, side_key = jax.random.split(key, 2)
    short_len = jax.random.randint(length_key, (SEQS, 1), 1, TOK_DEV)
    at_front = jax.random.randint(side_key, (SEQS, 1), 0, 2)
    positions = jnp.arange(GROUP, dtype=jnp.int32)[None, :]
    front_ids = (positions >= short_len).astype(jnp.int32)
    back_ids = (positions >= GROUP - short_len).astype(jnp.int32)
    return jnp.where(at_front == 1, front_ids, back_ids)


def steps_of(stream_key, dims, cuts, low, top_value):
    gain, own = 1.0, jax.random.fold_in(stream_key, 6)
    for dim, parts in cuts:
        steps = jnp.exp(jax.random.uniform(jax.random.fold_in(own, dim), (parts,), jnp.float32, low / len(cuts), top_value / len(cuts)))
        gain = gain * jnp.repeat(steps, dims[dim] // parts).reshape([-1 if axis == dim else 1 for axis in range(len(dims))])
    return gain


def gaussian(stream_key, extent, width, reach, cuts=(), held_as=jnp.bfloat16):
    values = jax.random.normal(stream_key, extent, jnp.float32) * width
    if len(cuts) > 0:
        values = steps_of(stream_key, extent, cuts, -0.22, 0.18) * values
    return jnp.clip(values, min=-reach, max=reach).astype(held_as)


def setup_inputs(seed: int = 0) -> dict:
    arg_keys = jax.random.split(jax.random.key(seed), 18)
    return {
        "tokens": gaussian(arg_keys[0], (SEQS, GROUP, D), 1.0, 6.0, ((0, 8), (1, 4))),
        "segments": draw_segments(jax.random.fold_in(arg_keys[17], 71), 0),
        "query_weight": gaussian(arg_keys[2], (D, D), D ** -0.5, 0.125, ((0, 8),)),
        "pair_weight": gaussian(arg_keys[3], (D, 2 * HD), D ** -0.5, 0.125, ((0, 8),)),
        "out_weight": gaussian(arg_keys[4], (D, D), (max(D // 256, 1)) ** -0.5, 2.0, ((0, 8),)),
        "query_bias": gaussian(arg_keys[5], (D,), 0.3, 1.5, ((0, 8),)),
        "value_bias": gaussian(arg_keys[6], (HD,), 0.3, 1.5, ((0, 8),)),
        "out_bias": gaussian(arg_keys[7], (D,), 0.3, 1.5, ((0, 8),)),
        "norm1_gain": jnp.clip(1.0 + 0.15 * jax.random.normal(arg_keys[8], (D,), jnp.float32), 0.25, 1.75).astype(jnp.bfloat16),
        "norm1_bias": gaussian(arg_keys[9], (D,), 0.3, 1.5, ((0, 8),)),
        "fc_weight": gaussian(arg_keys[10], (D, FF), D ** -0.5, 0.125, ((0, 8),)),
        "proj_weight": gaussian(arg_keys[11], (FF, D), (FF // 4) ** -0.5, 0.125, ((0, 8),)),
        "fc_bias": gaussian(arg_keys[12], (FF,), 0.3, 1.5, ((0, 8),)),
        "proj_bias": gaussian(arg_keys[13], (D,), 0.3, 1.5, ((0, 8),)),
        "norm2_gain": jnp.clip(1.0 + 0.15 * jax.random.normal(arg_keys[14], (D,), jnp.float32), 0.25, 1.75).astype(jnp.bfloat16),
        "norm2_bias": gaussian(arg_keys[15], (D,), 0.3, 1.5, ((0, 8),)),
        "cotangent": gaussian(arg_keys[16], (SEQS, GROUP, D), 1.0, 6.0, ((0, 8), (1, 4))),
    }


EPSILON = 1e-05
NEGATIVE = -1e+30
HIGHEST = lax.Precision.HIGHEST

@jax.custom_vjp
def low(v):
    return lax.optimization_barrier(v.astype(jnp.bfloat16)).astype(jnp.float32)

@jax.custom_vjp
def low_back(v):
    return v

def low_keep(v):
    return (low(v), None)

def low_pass(kept, grad):
    return (grad,)

def back_keep(v):
    return (v, None)

def back_low(kept, grad):
    return (low(grad),)
low.defvjp(low_keep, low_pass)
low_back.defvjp(back_keep, back_low)

def layer_norm(values_in, gain_vec, offset_vec):
    center = values_in - lax.optimization_barrier(jnp.mean(values_in, axis=-1, keepdims=True))
    spread = lax.optimization_barrier(jnp.mean(center * center, axis=-1, keepdims=True))
    return center * lax.rsqrt(spread + EPSILON) * gain_vec + offset_vec

def product(left_side, right_side):
    return jnp.dot(left_side, right_side, precision=HIGHEST, preferred_element_type=jnp.float32)

def attend(queries, key_rows, value_rows, seg_row):
    block_rows = math.gcd(GROUP, 512)
    positions = jnp.arange(GROUP, dtype=jnp.int32)
    scaling = 1.0 / math.sqrt(HD)

    def one_block(block_index):
        first_row = (block_index * block_rows).astype(jnp.int32)
        query_part = lax.dynamic_slice_in_dim(queries, first_row, block_rows, 0)
        query_pos = first_row + jnp.arange(block_rows, dtype=jnp.int32)
        query_seg = lax.dynamic_slice_in_dim(seg_row, first_row, block_rows, 0)
        allowed = (query_seg[:, None] == seg_row[None, :]) & (positions[None, :] <= query_pos[:, None])
        allowed = allowed & (query_pos[:, None] - positions[None, :] < WINDOW)
        scores = low_back(scaling * jnp.einsum('thd,kd->thk', query_part, key_rows, precision=HIGHEST))
        masked = jnp.where(allowed[:, None, :], scores, NEGATIVE)
        largest = lax.optimization_barrier(jnp.max(masked, axis=-1, keepdims=True))
        weights = jnp.where(allowed[:, None, :], jnp.exp(masked - largest), 0.0)
        probabilities = weights / lax.optimization_barrier(jnp.sum(weights, axis=-1, keepdims=True))
        return jnp.einsum('thk,kd->thd', low(probabilities), value_rows, precision=HIGHEST)
    pieces = lax.map(jax.checkpoint(one_block), jnp.arange(GROUP // block_rows, dtype=jnp.int32))
    return pieces.reshape(GROUP, H * HD)

def forward(tok_rows, seg_row, query_weight, pair_weight, out_weight, query_bias, value_bias, out_bias, norm1_gain, norm1_bias, fc_weight, proj_weight, fc_bias, proj_bias, norm2_gain, norm2_bias):
    normed_in = low(layer_norm(tok_rows, norm1_gain, norm1_bias))
    queries = low_back(low(product(normed_in, query_weight) + query_bias))
    pair_pre = product(normed_in, pair_weight)
    key_rows = low_back(low(pair_pre[:, :HD]))
    value_rows = low_back(low(pair_pre[:, HD:] + value_bias))
    attended = attend(queries.reshape(GROUP, H, HD), key_rows, value_rows, seg_row)
    attended = low_back(low(attended))
    middle = tok_rows + low_back(product(attended, out_weight) + out_bias)
    normed_mid = low(layer_norm(middle, norm2_gain, norm2_bias))
    hidden_pre = low_back(product(normed_mid, fc_weight) + fc_bias)
    hidden_act = low(jax.nn.gelu(hidden_pre, approximate=True))
    return middle + low_back(product(hidden_act, proj_weight) + proj_bias)

def reference(tokens, segments, query_weight, pair_weight, out_weight, query_bias, value_bias, out_bias, norm1_gain, norm1_bias, fc_weight, proj_weight, fc_bias, proj_bias, norm2_gain, norm2_bias, cotangent):
    params = tuple((argument.astype(jnp.float32) for argument in (query_weight, pair_weight, out_weight, query_bias, value_bias, out_bias, norm1_gain, norm1_bias, fc_weight, proj_weight, fc_bias, proj_bias, norm2_gain, norm2_bias)))

    def group_step(totals, inputs):
        tok_rows, seg_row, cot_rows = inputs

        def local_forward(rows_in, *weights):
            return forward(rows_in, seg_row, *weights)
        result, pull_back = jax.vjp(local_forward, tok_rows.astype(jnp.float32), *params)
        gradients = pull_back(cot_rows.astype(jnp.float32))
        totals = tuple((running + fresh for running, fresh in zip(totals, gradients[1:])))
        return (totals, (result.astype(jnp.bfloat16), gradients[0].astype(jnp.bfloat16)))
    zeros_init = tuple((jnp.zeros(argument.shape, jnp.float32) for argument in params))
    totals, (output, grad_tokens) = lax.scan(group_step, zeros_init, (tokens, segments, cotangent))
    return (output, grad_tokens, totals[0], totals[1], totals[2], totals[3], totals[4], totals[5], totals[6], totals[7], totals[8], totals[9], totals[10], totals[11], totals[12], totals[13])
```

```python
import math

import jax
import jax.numpy as jnp
from jax import lax
from jax.experimental import pallas as pl
from jax.experimental.pallas import tpu as pltpu
from jax.sharding import PartitionSpec as P

H = 16
HD = 128
WINDOW = 1024
EPSILON = 1e-05
NEGATIVE = -1e30
SCALING = 1.0 / math.sqrt(HD)
LOG2E = math.log2(math.e)
LOW = jnp.bfloat16
FULL = jnp.float32


def tie(value, *after):
    return lax.optimization_barrier((value, after))[0]


def product(left_side, right_side):
    return jnp.dot(left_side, right_side, preferred_element_type=FULL)


def product_tn(left_side, right_side):
    return lax.dot_general(
        left_side, right_side, (((0,), (0,)), ((), ())), preferred_element_type=FULL
    )


def product_nt(left_side, right_side):
    return lax.dot_general(
        left_side, right_side, (((1,), (1,)), ((), ())), preferred_element_type=FULL
    )


QUICK = pl.CostEstimate(flops=0, bytes_accessed=0, transcendentals=0)
ROOMY = pltpu.CompilerParams(vmem_limit_bytes=56 * 2**20)


def matmul(left_side, right_side, kind, step_rows=512, step_cols=2048, first=0, count=None):
    rows = count or (left_side.shape[1] if kind == "tn" else left_side.shape[0])
    depth = left_side.shape[0] if kind == "tn" else left_side.shape[1]
    cols = right_side.shape[0] if kind == "nt" else right_side.shape[1]
    step_rows, step_cols = math.gcd(step_rows, rows), math.gcd(step_cols, cols)
    inner = {"nn": product, "nt": product_nt, "tn": product_tn}[kind]
    at = first // step_rows

    def body(left_ref, right_ref, out_ref):
        out_ref[...] = inner(left_ref[...], right_ref[...]).astype(LOW)

    left_spec = (
        pl.BlockSpec((depth, step_rows), lambda j, i: (0, at + i))
        if kind == "tn"
        else pl.BlockSpec((step_rows, depth), lambda j, i: (at + i, 0))
    )
    right_spec = (
        pl.BlockSpec((step_cols, depth), lambda j, i: (j, 0))
        if kind == "nt"
        else pl.BlockSpec((depth, step_cols), lambda j, i: (0, j))
    )
    return pl.pallas_call(
        body,
        grid=(cols // step_cols, rows // step_rows),
        in_specs=[left_spec, right_spec],
        out_specs=pl.BlockSpec((step_rows, step_cols), lambda j, i: (i, j)),
        out_shape=jax.ShapeDtypeStruct((rows, cols), LOW),
        compiler_params=ROOMY,
        cost_estimate=QUICK,
        name="matmul_" + kind,
    )(left_side, right_side)


def member_order():
    return jnp.stack([member_of(k) for k in range(lax.axis_size("fsdp"))]).astype(jnp.int32)


def fc_gradient(mid_all, grad_part):
    peers = lax.axis_size("fsdp")
    rows, width = mid_all.shape
    step, cols = width // peers, grad_part.shape[1]

    def body(order_ref, mid_ref, grad_ref, out_ref):
        out_ref[0] = product_tn(mid_ref[...], grad_ref[...]).astype(LOW)

    return pl.pallas_call(
        body,
        grid_spec=pltpu.PrefetchScalarGridSpec(
            num_scalar_prefetch=1,
            grid=(peers,),
            in_specs=[
                pl.BlockSpec((rows, step), lambda k, order: (0, order[k])),
                pl.BlockSpec((rows, cols), lambda k, order: (0, 0)),
            ],
            out_specs=pl.BlockSpec((1, step, cols), lambda k, order: (k, 0, 0)),
        ),
        out_shape=jax.ShapeDtypeStruct((peers, step, cols), LOW),
        compiler_params=ROOMY,
        cost_estimate=QUICK,
        name="fc_gradient",
    )(member_order(), mid_all, grad_part)


def finish_rows(ends, pairs):
    rows, cols = pairs[0][0].shape
    step = rows // 2 if rows % 32 == 0 else rows

    def body(ends_ref, *refs):
        for c in range(len(pairs)):
            @pl.when(pl.program_id(0) == c)
            def _():
                chosen = jnp.where(ends_ref[0] == 1, refs[2 * c][...], refs[2 * c + 1][...])
                refs[-1][...] = chosen.astype(FULL)

    def spec(c):
        last = rows // step - 1
        return pl.BlockSpec(
            (step, cols), lambda i, j: (jnp.where(i == c, j, jnp.where(i > c, last, 0)), 0)
        )

    return pl.pallas_call(
        body,
        grid=(len(pairs), rows // step),
        in_specs=[pl.BlockSpec(memory_space=pltpu.SMEM)]
        + [spec(c) for c in range(len(pairs)) for unused in range(2)],
        out_specs=pl.BlockSpec((step, cols), lambda i, j: (i * (rows // step) + j, 0)),
        out_shape=jax.ShapeDtypeStruct((rows * len(pairs), cols), FULL),
        compiler_params=ROOMY,
        cost_estimate=QUICK,
        name="finish_rows",
    )(ends, *[array for pair in pairs for array in pair])


def finish_columns(ends, pairs, step):
    peers = lax.axis_size("fsdp")
    rows, cols = pairs[0][0].shape
    blocks = cols // step
    rounds = len(pairs) * blocks // peers

    def body(ends_ref, order_ref, *refs):
        for c in range(len(pairs)):
            @pl.when(pl.program_id(0) == c)
            def _():
                chosen = jnp.where(ends_ref[0] == 1, refs[2 * c][...], refs[2 * c + 1][...])
                refs[-1][...] = chosen.astype(FULL)

    def spec(c):
        return pl.BlockSpec(
            (rows, step),
            lambda i, j, ends, order: (0, jnp.where(i == c, j, jnp.where(i > c, blocks - 1, 0))),
        )

    def placed(i, j, ends, order):
        at = i * blocks + j
        return (0, order[lax.rem(at, peers)] * rounds + at // peers)

    return pl.pallas_call(
        body,
        grid_spec=pltpu.PrefetchScalarGridSpec(
            num_scalar_prefetch=2,
            grid=(len(pairs), blocks),
            in_specs=[spec(c) for c in range(len(pairs)) for unused in range(2)],
            out_specs=pl.BlockSpec((rows, step), placed),
        ),
        out_shape=jax.ShapeDtypeStruct((rows, cols * len(pairs)), FULL),
        compiler_params=ROOMY,
        cost_estimate=QUICK,
        name="finish_columns",
    )(ends, member_order(), *[array for pair in pairs for array in pair])


def feed_forward_body(mid_ref, fc_ref, bias_ref, cot_ref, proj_ref, hidden_ref, grad_ref):
    hidden_act, slope = gelu_pair(product(mid_ref[...], fc_ref[...]) + bias_ref[...])
    hidden_ref[...] = hidden_act.astype(LOW)
    grad_ref[...] = (product_nt(cot_ref[...], proj_ref[...]) * slope).astype(LOW)


def feed_forward(mid_all, fc_all, bias, cot_all, proj, first, count):
    rows, width = mid_all.shape
    step_rows, step = math.gcd(512, rows), math.gcd(512, count)
    at = first // step
    by_row = pl.BlockSpec((step_rows, width), lambda i, j: (i, 0))
    made = pl.BlockSpec((step_rows, step), lambda i, j: (i, j))
    return pl.pallas_call(
        feed_forward_body,
        grid=(rows // step_rows, count // step),
        in_specs=[
            by_row,
            pl.BlockSpec((width, step), lambda i, j: (0, at + j)),
            pl.BlockSpec((1, step), lambda i, j: (0, at + j)),
            by_row,
            pl.BlockSpec((step, width), lambda i, j: (at + j, 0)),
        ],
        out_specs=[made, made],
        out_shape=[jax.ShapeDtypeStruct((rows, count), LOW)] * 2,
        compiler_params=ROOMY,
        cost_estimate=QUICK,
        name="feed_forward",
    )(mid_all, fc_all, bias[None], cot_all, proj)


def by_xor():
    return lax.axis_size("fsdp") == 8


def swap(array, bits):
    return lax.ppermute(array, "fsdp", [(i, i ^ bits) for i in range(8)])


def member_of(k):
    return lax.axis_index("fsdp") ^ k if by_xor() else jnp.int32(k)


def near_rows(own):
    return swap(own, 2), swap(own, 4)


def gather_rows(own, near, whole):
    count = own.shape[0]
    half = count // 2
    along_x, along_y = near
    first_half, second_half = swap(along_x[:half], 4), swap(along_y[half:], 2)
    placed = [
        (0, 0, own),
        (1, 0, swap(own, 1)),
        (2, 0, along_x),
        (3, 0, swap(along_x, 1)),
        (4, 0, along_y),
        (5, 0, swap(along_y, 1)),
        (6, 0, first_half),
        (6, half, second_half),
        (7, 0, swap(first_half, 1)),
        (7, half, swap(second_half, 1)),
    ]
    for k, offset, block in placed:
        start = (member_of(k) * count + offset,) + (0,) * (own.ndim - 1)
        whole = lax.dynamic_update_slice(whole, block, start)
    return whole


def gather_plain(own):
    return lax.all_gather(own, "fsdp", axis=0, tiled=True)


def gather_small(own):
    held = own[None]
    for bits in (1, 2, 4):
        held = jnp.concatenate([held, swap(held, bits)], axis=0)
    return relative(held, 0)


def add_low(first, *others):
    total = first.astype(FULL)
    for other in others:
        total = total + other.astype(FULL)
    return total.astype(LOW)


def scatter_rows(array):
    return lax.psum_scatter(array, "fsdp", scatter_dimension=0, tiled=True)


def in_relative_order(array):
    step = array.shape[0] // lax.axis_size("fsdp")
    return [
        lax.dynamic_slice_in_dim(array, member_of(k) * step, step, 0)
        for k in range(lax.axis_size("fsdp"))
    ]


def scatter_first(blocks):
    if not by_xor():
        return blocks
    return [add_low(blocks[k], swap(blocks[k + 1], 1)) for k in (0, 2, 4, 6)]


def scatter_second(held):
    if not by_xor():
        return held
    mine, along_x, along_y, across = held
    half = mine.shape[0] // 2
    upper, lower = swap(across[:half], 2), swap(across[half:], 4)
    along_y = jnp.concatenate([add_low(along_y[:half], upper), along_y[half:]], axis=0)
    along_x = jnp.concatenate([along_x[:half], add_low(along_x[half:], lower)], axis=0)
    return [mine, along_x, along_y]


def scatter_third(held):
    if not by_xor():
        return scatter_rows(jnp.concatenate(held, axis=0)).astype(FULL)
    mine, along_x, along_y = held
    from_x, from_y = swap(along_x, 2), swap(along_y, 4)
    return mine.astype(FULL) + from_x.astype(FULL) + from_y.astype(FULL)


def exchange_blocks(blocks):
    if not by_xor():
        moved = lax.all_to_all(jnp.stack(blocks), "fsdp", 0, 0, tiled=True)
        return [moved[k] for k in range(len(blocks))]
    return [blocks[0]] + [swap(blocks[k], k) for k in range(1, 8)]


def relative(array, axis):
    if not by_xor():
        return array
    step = array.shape[axis] // 8
    return jnp.concatenate(
        [lax.dynamic_slice_in_dim(array, member_of(k) * step, step, axis) for k in range(8)],
        axis=axis,
    )


def columns_sent(own):
    planes = lax.axis_size("ctx")
    part, share = own.shape[0] // planes, own.shape[1] // 8
    place = lax.axis_index("ctx")
    return [
        lax.dynamic_slice(own, (place * part, member_of(k) * share), (part, share)) for k in range(8)
    ]


def columns_held(moved):
    held = jnp.zeros((8,) + moved[0].shape, moved[0].dtype)
    for k in range(8):
        held = lax.dynamic_update_slice(held, moved[k][None], (member_of(k), 0, 0))
    return held


def next_plane(held):
    planes = lax.axis_size("ctx")
    return lax.ppermute(held, "ctx", [(i, (i + 1) % planes) for i in range(planes)])


def columns_whole(held_parts):
    planes = len(held_parts)
    peers, part, share = held_parts[0].shape
    whole = jnp.zeros((peers, planes, part, share), held_parts[0].dtype)
    for step, held in enumerate(held_parts):
        source = lax.rem(lax.axis_index("ctx") + planes - step, planes)
        whole = lax.dynamic_update_slice(whole, held[:, None], (0, source, 0, 0))
    return whole.reshape(peers * planes * part, share)


def tick_body(at_end_ref, given, *refs):
    names = [name for name, there in given if there]
    held = dict(zip(names, refs))
    made = list(refs[len(names) :])

    def add(first, second):
        return (held[first][...].astype(FULL) + held[second][...].astype(FULL)).astype(LOW)

    if "fresh" in held:
        made.pop(0)[...] = add("fresh", "from_end")
    if "middle" in held:
        total = add("middle", "other")
        if "later" in held:
            total = jnp.where(at_end_ref[0] == 1, held["later"][...], total)
        made.pop(0)[...] = total


class SumOverCtx:
    def __init__(self, first):
        self.on_line = lax.axis_size("ctx") == 4
        place = lax.axis_index("ctx")
        self.ends = ((place == 0) | (place == 3)).astype(jnp.int32)[None]
        self.state = (first, None, None, first)
        self.results = []

    def combine(self, **arrays):
        given = {name: array for name, array in arrays.items() if array is not None}
        shape = next(iter(given.values())).shape
        count = ("fresh" in given) + ("middle" in given)
        pieces = 4 if shape[0] % 64 == 0 else 1
        spec = pl.BlockSpec((shape[0] // pieces, shape[1]), lambda i: (i, 0))
        flags = [(name, name in given) for name in arrays]
        return pl.pallas_call(
            lambda at_end_ref, *refs: tick_body(at_end_ref, flags, *refs),
            grid=(pieces,),
            in_specs=[pl.BlockSpec(memory_space=pltpu.SMEM)] + [spec] * len(given),
            out_specs=[spec] * count,
            out_shape=[jax.ShapeDtypeStruct(shape, LOW)] * count,
            compiler_params=ROOMY,
            cost_estimate=QUICK,
            name="tick",
        )(self.ends, *given.values())

    def move(self, later=None):
        fresh, middle, outgoing, incoming = self.state
        if not self.on_line:
            if fresh is not None:
                total = lax.psum(fresh, "ctx")
                self.results.append((total, total))
            self.state = (later, None, None, None)
            return
        inward, outward = [(0, 1), (3, 2)], [(1, 0), (2, 3)]
        from_end = other = None
        if outgoing is not None and outgoing is incoming:
            from_end = from_middle = lax.ppermute(outgoing, "ctx", inward + outward)
        else:
            if fresh is not None:
                from_end = lax.ppermute(incoming, "ctx", inward)
            if outgoing is not None:
                from_middle = lax.ppermute(outgoing, "ctx", outward)
        if outgoing is not None:
            self.results.append((from_middle, outgoing))
        if middle is not None:
            other = lax.ppermute(middle, "ctx", [(1, 2), (2, 1)])
        pair_sum = total = None
        joined = middle is not None and later is not None and later.shape == middle.shape
        alike = fresh is None or middle is None or fresh.shape == middle.shape
        chosen = later if joined else None
        if alike and (fresh is not None or middle is not None):
            made = self.combine(
                fresh=fresh, from_end=from_end, middle=middle, other=other, later=chosen
            )
            pair_sum = made[0] if fresh is not None else None
            total = made[-1] if middle is not None else None
        elif fresh is not None:
            (pair_sum,) = self.combine(fresh=fresh, from_end=from_end)
            (total,) = self.combine(middle=middle, other=other, later=chosen)
        self.state = (later, pair_sum, total, total if joined else later)

    def fence(self, *values):
        fresh, middle, outgoing, incoming = self.state
        joined = outgoing is not None and outgoing is incoming
        held = (fresh, middle, outgoing, None if joined or incoming is fresh else incoming)
        held, values = lax.optimization_barrier((held, values))
        incoming = held[2] if joined else held[0]
        self.state = (held[0], held[1], held[2], incoming)
        return values


def attend_kernel(query_ref, key_ref, value_t_ref, mask_ref, out_ref, total_ref):
    scores = product_nt(key_ref[...], query_ref[...]) * (SCALING * LOG2E) + mask_ref[...]
    largest = jnp.max(scores, axis=0, keepdims=True)
    weights = jnp.exp2(scores - largest)
    weight_sum = jnp.sum(weights, axis=0, keepdims=True)
    gathered = product(value_t_ref[...], weights.astype(LOW))
    out_ref[...] = (gathered / weight_sum).T.astype(LOW)
    total_ref[0] = largest + jnp.log2(weight_sum)


def attend(queries, keys, values_t, mask):
    rows, key_rows = queries.shape[0], keys.shape[0]
    whole = lambda head: (0, 0)
    by_head = lambda head: (0, head)
    return pl.pallas_call(
        attend_kernel,
        grid=(H,),
        in_specs=[
            pl.BlockSpec((rows, HD), by_head),
            pl.BlockSpec((key_rows, HD), whole),
            pl.BlockSpec((HD, key_rows), whole),
            pl.BlockSpec((key_rows, rows), whole),
        ],
        out_specs=[
            pl.BlockSpec((rows, HD), by_head),
            pl.BlockSpec((1, 1, rows), lambda head: (head, 0, 0)),
        ],
        out_shape=[
            jax.ShapeDtypeStruct((rows, H * HD), LOW),
            jax.ShapeDtypeStruct((H, 1, rows), FULL),
        ],
        compiler_params=ROOMY,
        cost_estimate=QUICK,
        name="attend",
    )(queries, keys, values_t, mask)


def attend_back_kernel(
    query_ref,
    grad_ref,
    out_ref,
    total_ref,
    key_ref,
    key_t_ref,
    value_ref,
    mask_ref,
    grad_query_ref,
    grad_key_ref,
    grad_value_ref,
):
    @pl.when(pl.program_id(0) == 0)
    def _():
        grad_key_ref[...] = jnp.zeros_like(grad_key_ref)
        grad_value_ref[...] = jnp.zeros_like(grad_value_ref)

    query, grad = query_ref[...], grad_ref[...]
    scores = product_nt(key_ref[...], query) * (SCALING * LOG2E) + mask_ref[...]
    probs = jnp.exp2(scores - total_ref[0])
    grad_probs = product_nt(value_ref[...], grad)
    delta = jnp.sum((grad.astype(FULL) * out_ref[...].astype(FULL)).T, axis=0, keepdims=True)
    grad_scores = (probs * (grad_probs - delta)).astype(LOW)
    grad_value_ref[...] += product(probs.astype(LOW), grad)
    grad_key_ref[...] += product(grad_scores, query)
    grad_query_ref[...] = (product(key_t_ref[...], grad_scores).T * SCALING).astype(LOW)


def attend_back(queries, grad_out, out, totals, keys, keys_t, values, mask):
    rows, key_rows = queries.shape[0], keys.shape[0]
    whole = lambda head: (0, 0)
    by_head = lambda head: (0, head)
    return pl.pallas_call(
        attend_back_kernel,
        grid=(H,),
        in_specs=[
            pl.BlockSpec((rows, HD), by_head),
            pl.BlockSpec((rows, HD), by_head),
            pl.BlockSpec((rows, HD), by_head),
            pl.BlockSpec((1, 1, rows), lambda head: (head, 0, 0)),
            pl.BlockSpec((key_rows, HD), whole),
            pl.BlockSpec((HD, key_rows), whole),
            pl.BlockSpec((key_rows, HD), whole),
            pl.BlockSpec((key_rows, rows), whole),
        ],
        out_specs=[
            pl.BlockSpec((rows, HD), by_head),
            pl.BlockSpec((key_rows, HD), whole),
            pl.BlockSpec((key_rows, HD), whole),
        ],
        out_shape=[
            jax.ShapeDtypeStruct((rows, H * HD), LOW),
            jax.ShapeDtypeStruct((key_rows, HD), FULL),
            jax.ShapeDtypeStruct((key_rows, HD), FULL),
        ],
        compiler_params=ROOMY,
        cost_estimate=QUICK,
        name="attend_back",
    )(queries, grad_out, out, totals, keys, keys_t, values, mask)


def normalize(values_in):
    center = values_in - jnp.mean(values_in, axis=-1, keepdims=True)
    spread = jnp.mean(center * center, axis=-1, keepdims=True)
    inverse = lax.rsqrt(spread + EPSILON)
    return center * inverse, inverse


def norm_pullback(normed, inverse, gain_vec, grad_in):
    weighted = grad_in * gain_vec
    grad_values = inverse * (
        weighted
        - jnp.mean(weighted, axis=-1, keepdims=True)
        - normed * jnp.mean(weighted * normed, axis=-1, keepdims=True)
    )
    return grad_values, jnp.sum(grad_in * normed, axis=0), jnp.sum(grad_in, axis=0)


def gelu_pair(values_in):
    root = math.sqrt(2.0 / math.pi)
    square = values_in * values_in
    turned = jnp.tanh(root * values_in * (1.0 + 0.044715 * square))
    slope = 0.5 * (1.0 + turned) + 0.5 * values_in * (1.0 - turned * turned) * root * (
        1.0 + 3.0 * 0.044715 * square
    )
    return 0.5 * values_in * (1.0 + turned), slope


def per_device(
    tokens,
    segments,
    query_weight,
    pair_weight,
    out_weight,
    query_bias,
    value_bias,
    out_bias,
    norm1_gain,
    norm1_bias,
    fc_weight,
    proj_weight,
    fc_bias,
    proj_bias,
    norm2_gain,
    norm2_bias,
    cotangent,
):
    rows, width = tokens.shape[1:]
    peers = lax.axis_size("fsdp")
    depth_share = width // peers
    ctx_count = lax.axis_size("ctx")
    ctx_index = lax.axis_index("ctx")
    members = range(peers)

    spelled = by_xor() and ctx_count == 4
    ff_share = fc_weight.shape[1] // peers
    cot_own = cotangent[0]
    vectors = [query_bias, out_bias, norm1_gain, norm1_bias, proj_bias, norm2_gain, norm2_bias]
    vectors_own = jnp.concatenate(vectors + [value_bias])
    attn_weight = jnp.concatenate([query_weight, pair_weight], axis=1)
    attn_all = gather_plain(attn_weight)
    if spelled:
        packed = gather_small(vectors_own)
        held = columns_held(exchange_blocks(columns_sent(fc_weight)))
        blank_out, blank_mid = jnp.zeros((2, peers * depth_share, width), LOW)
        packed, held, blank_out, blank_mid = lax.optimization_barrier(
            (packed, held, blank_out, blank_mid)
        )
        out_near = near_rows(tie(out_weight, packed))
        held_parts = [held, next_plane(held)]
        out_near, held_parts, cot_sent = lax.optimization_barrier(
            (out_near, held_parts, cot_own)
        )
        out_all = gather_rows(out_weight, out_near, blank_out)
    else:
        packed = lax.all_gather(vectors_own, "fsdp", axis=0)
        out_all = gather_plain(out_weight)
        fc_all = lax.all_to_all(fc_weight, "fsdp", 1, 0, tiled=True)
    small = [
        packed[:, i * depth_share : (i + 1) * depth_share].reshape(-1).astype(FULL)
        for i in range(len(vectors))
    ]
    query_bias_all, out_bias_all, gain1, bias1, proj_bias_all, gain2, bias2 = small
    value_bias_all = packed[:, len(vectors) * depth_share :].reshape(-1).astype(FULL)

    tok_rows = tokens[0].astype(FULL)
    normed1, inverse1 = normalize(tok_rows)
    normed_in = (normed1 * gain1 + bias1).astype(LOW)
    attn_bias = jnp.concatenate([query_bias_all, jnp.zeros((HD,), FULL), value_bias_all])
    projected = (product(normed_in, attn_all) + attn_bias).astype(LOW)
    queries, pair_own = projected[:, :width], projected[:, width:]
    reach = min(ctx_count - 1, -(-(WINDOW - 1) // rows))
    pairs = [pair_own] + [
        lax.ppermute(pair_own, "ctx", [(i, i + d) for i in range(ctx_count - d)])
        for d in range(1, reach + 1)
    ]
    if spelled:
        held_parts, pairs, out_all, cot_sent = lax.optimization_barrier(
            (held_parts, pairs, out_all, cot_sent)
        )
        held_parts = held_parts + [next_plane(held_parts[-1])]
        cot_all = gather_plain(cot_sent)
    else:
        cot_all = gather_plain(cot_own)
    pair_rows = jnp.concatenate(pairs, axis=0)
    seg_row = segments[0]
    query_first = ctx_index * rows
    key_pos = jnp.concatenate(
        [query_first - d * rows + jnp.arange(rows, dtype=jnp.int32) for d in range(reach + 1)]
    )
    query_pos = query_first + jnp.arange(rows, dtype=jnp.int32)
    query_seg = lax.dynamic_slice_in_dim(seg_row, query_first, rows, 0)
    key_seg = jnp.concatenate(
        [
            lax.dynamic_slice_in_dim(seg_row, jnp.maximum(query_first - d * rows, 0), rows, 0)
            for d in range(reach + 1)
        ]
    )
    allowed = (
        (key_seg[:, None] == query_seg[None, :])
        & (key_pos[:, None] <= query_pos[None, :])
        & (query_pos[None, :] - key_pos[:, None] < WINDOW)
        & (key_pos[:, None] >= 0)
    )
    mask = jnp.where(allowed, 0.0, NEGATIVE).astype(FULL)
    keys, values = pair_rows[:, :HD], pair_rows[:, HD:]
    attended, score_totals = attend(queries, keys, values.T, mask)
    middle = tok_rows + (product(attended, out_all) + out_bias_all)
    normed2, inverse2 = normalize(middle)
    normed_mid = (normed2 * gain2 + bias2).astype(LOW)

    if spelled:
        held_parts, normed_mid = lax.optimization_barrier((held_parts, normed_mid))
        held_parts = held_parts + [next_plane(held_parts[-1])]
        fc_all = columns_whole(held_parts)
        mid_all = gather_rows(normed_mid, near_rows(normed_mid), blank_mid)
    else:
        mid_all = gather_plain(normed_mid)
    fc_bias_own = fc_bias.astype(FULL)
    half = ff_share // 2
    piece = half // 2
    ff_args = (mid_all, fc_all, fc_bias_own, cot_all, proj_weight)
    hidden_first, grad_first = feed_forward(*ff_args, 0, half)

    def proj_term(hidden_part, first):
        return matmul(hidden_part, cot_all, "tn", 256, 1024, first, piece)

    sums = SumOverCtx(proj_term(hidden_first, 0))
    mid_all, cot_all, fc_all, hidden_first, grad_first = sums.fence(
        mid_all, cot_all, fc_all, hidden_first, grad_first
    )

    ff_args = (mid_all, fc_all, fc_bias_own, cot_all, proj_weight)
    hidden_second, grad_second = feed_forward(*ff_args, half, half)
    sums.move(proj_term(hidden_first, piece))
    mid_all, cot_all, grad_first, grad_second, hidden_first, hidden_second = sums.fence(
        mid_all, cot_all, grad_first, grad_second, hidden_first, hidden_second
    )

    grad_pre = jnp.concatenate([grad_first, grad_second], axis=1)
    grad_mid_part = matmul(grad_pre, fc_all, "nt")
    sums.move(proj_term(hidden_second, 0))
    mid_all, cot_all, grad_first, grad_second, hidden_second, grad_mid_part = sums.fence(
        mid_all, cot_all, grad_first, grad_second, hidden_second, grad_mid_part
    )

    grad_normed_mid = scatter_rows(grad_mid_part)
    fc_first = fc_gradient(mid_all, grad_first)
    fc_second = fc_gradient(mid_all, grad_second)
    sums.move(proj_term(hidden_second, piece))
    grad_first, grad_second, hidden_second, fc_first, fc_second = sums.fence(
        grad_first, grad_second, hidden_second, fc_first, fc_second
    )

    hidden = jnp.concatenate([hidden_first, hidden_second], axis=1)
    out_part = matmul(hidden, proj_weight, "nn")
    fc_first = exchange_blocks([fc_first[k] for k in members])
    group = peers // 2
    sums.move(jnp.concatenate(fc_first[:group], axis=1))
    fc_first, fc_second, out_part, grad_normed_mid = sums.fence(
        fc_first, fc_second, out_part, grad_normed_mid
    )

    fc_second = exchange_blocks([fc_second[k] for k in members])
    grad_middle_ln, grad_gain2, grad_bias2 = norm_pullback(
        normed2, inverse2, gain2, grad_normed_mid
    )
    grad_middle = cot_own.astype(FULL) + grad_middle_ln
    grad_mid_low = grad_middle.astype(LOW)
    grad_attended = product_nt(grad_mid_low, out_all).astype(LOW)
    out_term = product_tn(attended, grad_mid_low).astype(LOW)
    sums.move(jnp.concatenate(fc_first[group:], axis=1))
    fc_second, grad_middle, grad_mid_low, grad_attended, out_term = sums.fence(
        fc_second, grad_middle, grad_mid_low, grad_attended, out_term
    )

    out_share = scatter_rows(out_term)
    grad_query_low, grad_keys, grad_values = attend_back(
        queries, grad_attended, attended, score_totals, keys, keys.T, values, mask
    )
    sums.move(jnp.concatenate(fc_second[:group], axis=1))
    fc_second, grad_middle, grad_mid_low, grad_query_low, grad_keys, grad_values = sums.fence(
        fc_second, grad_middle, grad_mid_low, grad_query_low, grad_keys, grad_values
    )

    grad_pairs = jnp.concatenate([grad_keys, grad_values], axis=1)
    grad_pair = grad_pairs[:rows]
    for d in range(1, reach + 1):
        sent = grad_pairs[d * rows : (d + 1) * rows].astype(LOW)
        grad_pair = grad_pair + lax.ppermute(
            sent, "ctx", [(i + d, i) for i in range(ctx_count - d)]
        ).astype(FULL)
    pair_scaling = jnp.concatenate([jnp.full((HD,), SCALING, FULL), jnp.ones((HD,), FULL)])
    grad_pair_low = (grad_pair * pair_scaling).astype(LOW)
    grad_projected = jnp.concatenate([grad_query_low, grad_pair_low], axis=1)
    fc_second, grad_middle, grad_mid_low, grad_projected = sums.fence(
        fc_second, grad_middle, grad_mid_low, grad_projected
    )

    attn_term = product_tn(normed_in, grad_projected).astype(LOW)
    sums.move(jnp.concatenate(fc_second[group:], axis=1))
    grad_middle, grad_mid_low, grad_projected, attn_term = sums.fence(
        grad_middle, grad_mid_low, grad_projected, attn_term
    )

    attn_held = scatter_first(in_relative_order(attn_term))
    attn_held = scatter_second(attn_held)
    grad_normed_in = product_nt(grad_projected, attn_all)
    sums.move(out_share)
    grad_middle, grad_mid_low, grad_projected, attn_held, grad_normed_in = sums.fence(
        grad_middle, grad_mid_low, grad_projected, attn_held, grad_normed_in
    )

    attn_share = scatter_third(attn_held).astype(LOW)
    grad_tok_ln, grad_gain1, grad_bias1 = norm_pullback(normed1, inverse1, gain1, grad_normed_in)
    grad_tokens = (grad_middle + grad_tok_ln).astype(LOW)
    grad_projected_bias = jnp.sum(grad_projected.astype(FULL), axis=0)
    vector_terms = [
        grad_projected_bias[:width],
        jnp.sum(grad_mid_low.astype(FULL), axis=0),
        grad_gain1,
        grad_bias1,
        jnp.sum(cot_own.astype(FULL), axis=0),
        grad_gain2,
        grad_bias2,
    ]
    by_member = jnp.concatenate(
        [term.reshape(peers, depth_share) for term in vector_terms]
        + [grad_projected_bias[width + HD :].reshape(peers, HD // peers)],
        axis=1,
    )
    used = by_member.shape[1]
    by_member = jnp.pad(by_member, ((0, 0), (0, -used % 256))).reshape(peers, -1, 256)
    vector_rows = by_member.shape[1]
    by_member = jnp.pad(by_member, ((0, 0), (0, -vector_rows % 16), (0, 0))).astype(LOW)
    vector_pad = by_member.shape[1]
    vector_held = scatter_first(in_relative_order(by_member.reshape(peers * vector_pad, 256)))
    sums.move(attn_share[:, :width])
    vector_held, attn_share = sums.fence(vector_held, attn_share)

    vector_share = scatter_third(scatter_second(vector_held)).astype(LOW)
    grad_fc_bias = jnp.concatenate(
        [jnp.sum(part.astype(FULL), axis=0) for part in (grad_first, grad_second)]
    )
    fc_bias_rows = grad_fc_bias.astype(LOW).reshape(-1, 256)
    fc_rows = fc_bias_rows.shape[0]
    fc_bias_rows = jnp.pad(fc_bias_rows, ((0, -fc_rows % 16), (0, 0)))
    pair_share = attn_share[:, width:]
    sums.move(jnp.concatenate([pair_share, vector_share, fc_bias_rows], axis=0))
    (out_part,) = sums.fence(out_part)

    out_sum = scatter_rows(out_part).astype(FULL)
    output = (middle + (out_sum + proj_bias_all)).astype(LOW)
    sums.move()
    sums.fence()
    sums.move()
    sums.fence()
    sums.move()

    grad_proj = finish_rows(sums.ends, sums.results[:4])
    grad_fc = finish_columns(sums.ends, sums.results[4:8], half)
    grad_out, grad_query, last = [
        jnp.where(sums.ends[0] == 1, at_end, inside).astype(FULL)
        for at_end, inside in sums.results[8:]
    ]
    pair_count = pair_share.shape[0]
    vector_sum = last[pair_count : pair_count + vector_rows].reshape(-1)
    fc_at = pair_count + vector_share.shape[0]
    grad_fc_bias = last[fc_at : fc_at + fc_rows].reshape(-1)
    shares = [vector_sum[i * depth_share : (i + 1) * depth_share] for i in range(len(vectors))]
    value_share = vector_sum[len(vectors) * depth_share : used]
    return (
        output[None],
        grad_tokens[None],
        grad_query,
        last[:pair_count],
        grad_out,
        shares[0],
        value_share,
        shares[1],
        shares[2],
        shares[3],
        grad_fc,
        grad_proj,
        grad_fc_bias,
        shares[4],
        shares[5],
        shares[6],
    )


def solution(mesh):
    weight, vector, token = P("fsdp", None), P("fsdp"), P("fsdp", "ctx", None)
    return jax.shard_map(
        per_device,
        mesh=mesh,
        in_specs=(
            token,
            weight,
            weight,
            weight,
            weight,
            vector,
            vector,
            vector,
            vector,
            vector,
            weight,
            weight,
            vector,
            vector,
            vector,
            vector,
            token,
        ),
        out_specs=(
            token,
            token,
            weight,
            weight,
            weight,
            vector,
            vector,
            vector,
            vector,
            vector,
            weight,
            weight,
            vector,
            vector,
            vector,
            vector,
        ),
        check_vma=False,
    )
```

```python
import math

import jax
import jax.numpy as jnp
from jax import lax
from jax.experimental import pallas as pl
from jax.experimental.pallas import tpu as pltpu
from jax.sharding import PartitionSpec as P

H = 16
HD = 128
WINDOW = 1024
EPSILON = 1e-05
NEGATIVE = -1e30
SCALING = 1.0 / math.sqrt(HD)
LOG2E = math.log2(math.e)
LOW = jnp.bfloat16
FULL = jnp.float32


def tie(value, *after):
    return lax.optimization_barrier((value, after))[0]


def product(left_side, right_side):
    return jnp.dot(left_side, right_side, preferred_element_type=FULL)


def product_tn(left_side, right_side):
    return lax.dot_general(
        left_side, right_side, (((0,), (0,)), ((), ())), preferred_element_type=FULL
    )


def product_nt(left_side, right_side):
    return lax.dot_general(
        left_side, right_side, (((1,), (1,)), ((), ())), preferred_element_type=FULL
    )


QUICK = pl.CostEstimate(flops=0, bytes_accessed=0, transcendentals=0)
ROOMY = pltpu.CompilerParams(vmem_limit_bytes=56 * 2**20)


def matmul(
    left_side,
    right_side,
    kind,
    step_rows=512,
    step_cols=2048,
    first=0,
    count=None,
    out_type=LOW,
):
    rows = count or (left_side.shape[1] if kind == "tn" else left_side.shape[0])
    depth = left_side.shape[0] if kind == "tn" else left_side.shape[1]
    cols = right_side.shape[0] if kind == "nt" else right_side.shape[1]
    step_rows, step_cols = math.gcd(step_rows, rows), math.gcd(step_cols, cols)
    inner = {"nn": product, "nt": product_nt, "tn": product_tn}[kind]
    at = first // step_rows

    def body(left_ref, right_ref, out_ref):
        out_ref[...] = inner(left_ref[...], right_ref[...]).astype(out_type)

    left_spec = (
        pl.BlockSpec((depth, step_rows), lambda j, i: (0, at + i))
        if kind == "tn"
        else pl.BlockSpec((step_rows, depth), lambda j, i: (at + i, 0))
    )
    right_spec = (
        pl.BlockSpec((step_cols, depth), lambda j, i: (j, 0))
        if kind == "nt"
        else pl.BlockSpec((depth, step_cols), lambda j, i: (0, j))
    )
    return pl.pallas_call(
        body,
        grid=(cols // step_cols, rows // step_rows),
        in_specs=[left_spec, right_spec],
        out_specs=pl.BlockSpec((step_rows, step_cols), lambda j, i: (i, j)),
        out_shape=jax.ShapeDtypeStruct((rows, cols), out_type),
        compiler_params=ROOMY,
        cost_estimate=QUICK,
        name="matmul_" + kind,
    )(left_side, right_side)


def member_order():
    return jnp.stack([member_of(k) for k in range(lax.axis_size("fsdp"))]).astype(jnp.int32)


def fc_gradient(mid_all, grad_pre):
    peers = lax.axis_size("fsdp")
    rows, width = mid_all.shape
    step, cols = width // peers, grad_pre.shape[1]

    def body(order_ref, mid_ref, grad_ref, out_ref):
        out_ref[0] = product_tn(mid_ref[...], grad_ref[...]).astype(LOW)

    return pl.pallas_call(
        body,
        grid_spec=pltpu.PrefetchScalarGridSpec(
            num_scalar_prefetch=1,
            grid=(peers,),
            in_specs=[
                pl.BlockSpec((rows, step), lambda k, order: (0, order[k])),
                pl.BlockSpec((rows, cols), lambda k, order: (0, 0)),
            ],
            out_specs=pl.BlockSpec((1, step, cols), lambda k, order: (k, 0, 0)),
        ),
        out_shape=jax.ShapeDtypeStruct((peers, step, cols), LOW),
        compiler_params=ROOMY,
        cost_estimate=QUICK,
        name="fc_gradient",
    )(member_order(), mid_all, grad_pre)


def attn_gradient(normed_in, grad_projected, extra):
    peers = lax.axis_size("fsdp")
    rows, width = normed_in.shape
    step, cols, more = width // peers, grad_projected.shape[1], extra.shape[1]

    def body(normed_ref, grad_ref, extra_ref, out_ref):
        out_ref[0, :step] = product_tn(normed_ref[...], grad_ref[...]).astype(LOW)
        out_ref[0, step:] = extra_ref[0]

    return pl.pallas_call(
        body,
        grid=(peers,),
        in_specs=[
            pl.BlockSpec((rows, step), lambda k: (0, k)),
            pl.BlockSpec((rows, cols), lambda k: (0, 0)),
            pl.BlockSpec((1, more, cols), lambda k: (k, 0, 0)),
        ],
        out_specs=pl.BlockSpec((1, step + more, cols), lambda k: (k, 0, 0)),
        out_shape=jax.ShapeDtypeStruct((peers, step + more, cols), LOW),
        compiler_params=ROOMY,
        cost_estimate=QUICK,
        name="attn_gradient",
    )(normed_in, grad_projected, extra)


def finish(ends, pairs, across, parts=1):
    rows, cols = pairs[0][0].shape
    step = cols // parts

    def body(ends_ref, order_ref, *refs):
        for c in range(len(pairs)):
            @pl.when(pl.program_id(0) == c)
            def _():
                for j in range(parts):
                    at = (slice(None), slice(j * step, (j + 1) * step))
                    chosen = jnp.where(ends_ref[0] == 1, refs[2 * c][at], refs[2 * c + 1][at])
                    place = j
                    if parts > 1:
                        place = lax.rem(order_ref[(c % across) * parts + j], parts)
                    start = pl.multiple_of(place * step, step)
                    refs[-1][:, pl.ds(start, step)] = chosen.astype(FULL)

    def placed(c, ends, order):
        row, at = c // across, lax.rem(c, across)
        return (row, order[at * parts] // parts if parts > 1 else at)

    whole = pl.BlockSpec((rows, cols), lambda c, ends, order: (0, 0))
    return pl.pallas_call(
        body,
        grid_spec=pltpu.PrefetchScalarGridSpec(
            num_scalar_prefetch=2,
            grid=(len(pairs),),
            in_specs=[whole] * (2 * len(pairs)),
            out_specs=pl.BlockSpec((rows, cols), placed),
        ),
        out_shape=jax.ShapeDtypeStruct((rows * len(pairs) // across, cols * across), FULL),
        compiler_params=ROOMY,
        cost_estimate=QUICK,
        name="finish",
    )(ends, member_order(), *[array for pair in pairs for array in pair])


def feed_forward_body(mid_ref, fc_ref, bias_ref, cot_ref, proj_ref, hidden_ref, grad_ref):
    hidden_act, slope = gelu_pair(product(mid_ref[...], fc_ref[...]) + bias_ref[...])
    hidden_ref[...] = hidden_act.astype(LOW)
    grad_ref[...] = (product_nt(cot_ref[...], proj_ref[...]) * slope).astype(LOW)


def feed_forward(mid_all, fc_all, bias, cot_all, proj, part, made=None):
    rows, width = mid_all.shape
    cols = fc_all.shape[1]
    step_rows, step = math.gcd(512, rows), cols // 2
    by_row = pl.BlockSpec((step_rows, width), lambda i: (i, 0))
    placed = pl.BlockSpec((step_rows, step), lambda i: (i, part))
    held = [] if made is None else list(made)

    def body(*refs):
        feed_forward_body(*refs[:5], *refs[-2:])

    return pl.pallas_call(
        body,
        grid=(rows // step_rows,),
        in_specs=[
            by_row,
            pl.BlockSpec((width, step), lambda i: (0, part)),
            pl.BlockSpec((1, step), lambda i: (0, part)),
            by_row,
            pl.BlockSpec((step, width), lambda i: (part, 0)),
        ]
        + [pl.BlockSpec(memory_space=pl.ANY)] * len(held),
        out_specs=[placed, placed],
        out_shape=[jax.ShapeDtypeStruct((rows, cols), LOW)] * 2,
        input_output_aliases={5: 0, 6: 1} if held else {},
        compiler_params=ROOMY,
        cost_estimate=QUICK,
        name="feed_forward",
    )(mid_all, fc_all, bias[None], cot_all, proj, *held)


def by_xor():
    return lax.axis_size("fsdp") == 8


def swap(array, bits):
    return lax.ppermute(array, "fsdp", [(i, i ^ bits) for i in range(8)])


def member_of(k):
    return lax.axis_index("fsdp") ^ k if by_xor() else jnp.int32(k)


def near_rows(own):
    return swap(own, 2), swap(own, 4)


def placed_own(own):
    def body(order_ref, own_ref, out_ref):
        out_ref[...] = own_ref[...]

    return pl.pallas_call(
        body,
        grid_spec=pltpu.PrefetchScalarGridSpec(
            num_scalar_prefetch=1,
            grid=(1,),
            in_specs=[pl.BlockSpec(own.shape, lambda k, order: (0, 0))],
            out_specs=pl.BlockSpec(own.shape, lambda k, order: (order[0], 0)),
        ),
        out_shape=jax.ShapeDtypeStruct((8 * own.shape[0], own.shape[1]), own.dtype),
        compiler_params=ROOMY,
        cost_estimate=QUICK,
        name="placed_own",
    )(member_order(), own)


def gather_rows(own, near):
    count = own.shape[0]
    half = count // 2
    along_x, along_y = near
    first_half, second_half = swap(along_x[:half], 4), swap(along_y[half:], 2)
    placed = [
        (1, 0, swap(own, 1)),
        (2, 0, along_x),
        (4, 0, along_y),
        (3, 0, swap(along_x, 1)),
        (5, 0, swap(along_y, 1)),
        (6, 0, first_half),
        (6, half, second_half),
        (7, 0, swap(first_half, 1)),
        (7, half, swap(second_half, 1)),
    ]
    whole = placed_own(own)
    for k, offset, block in placed:
        whole = lax.dynamic_update_slice(whole, block, (member_of(k) * count + offset, 0))
    return whole


def gather_plain(own):
    return lax.all_gather(own, "fsdp", axis=0, tiled=True)


def gather_small(own):
    held = own[None]
    for bits in (1, 2, 4):
        held = jnp.concatenate([held, swap(held, bits)], axis=0)
    return relative(held, 0)


def scatter_rows(array):
    return lax.psum_scatter(array, "fsdp", scatter_dimension=0, tiled=True)


def exchange_blocks(blocks):
    if not by_xor():
        moved = lax.all_to_all(jnp.stack(blocks), "fsdp", 0, 0, tiled=True)
        return [moved[k] for k in range(len(blocks))]
    moved = {0: blocks[0]}
    for k in (2, 4, 6, 1, 3, 5, 7):
        moved[k] = swap(blocks[k], k)
    return [moved[k] for k in range(8)]


def relative(array, axis):
    if not by_xor():
        return array
    step = array.shape[axis] // 8
    return jnp.concatenate(
        [lax.dynamic_slice_in_dim(array, member_of(k) * step, step, axis) for k in range(8)],
        axis=axis,
    )


def columns_sent(own):
    planes = lax.axis_size("ctx")
    part, share = own.shape[0] // planes, own.shape[1] // 8
    place = lax.axis_index("ctx")
    return [
        lax.dynamic_slice(own, (place * part, member_of(k) * share), (part, share)) for k in range(8)
    ]


def columns_held(moved):
    held = jnp.zeros((8,) + moved[0].shape, moved[0].dtype)
    for k in range(8):
        held = lax.dynamic_update_slice(held, moved[k][None], (member_of(k), 0, 0))
    return held


def next_plane(held):
    planes = lax.axis_size("ctx")
    return lax.ppermute(held, "ctx", [(i, (i + 1) % planes) for i in range(planes)])


def columns_whole(held_parts):
    planes = len(held_parts)
    peers, part, share = held_parts[0].shape
    whole = jnp.zeros((peers, planes, part, share), held_parts[0].dtype)
    for step, held in enumerate(held_parts):
        source = lax.rem(lax.axis_index("ctx") + planes - step, planes)
        whole = lax.dynamic_update_slice(whole, held[:, None], (0, source, 0, 0))
    return whole.reshape(peers * planes * part, share)


def tick_body(at_end_ref, given, *refs):
    names = [name for name, there in given if there]
    held = dict(zip(names, refs))
    made = list(refs[len(names) :])

    def add(first, second):
        return (held[first][...].astype(FULL) + held[second][...].astype(FULL)).astype(LOW)

    if "fresh" in held:
        made.pop(0)[...] = add("fresh", "from_end")
    if "middle" in held:
        total = add("middle", "other")
        if "later" in held:
            total = jnp.where(at_end_ref[0] == 1, held["later"][...], total)
        made.pop(0)[...] = total


class SumOverCtx:
    def __init__(self, first):
        self.on_line = lax.axis_size("ctx") == 4
        place = lax.axis_index("ctx")
        self.ends = ((place == 0) | (place == 3)).astype(jnp.int32)[None]
        self.state = (first, None, None, first)
        self.results = []
        self.fenced = 0

    def combine(self, **arrays):
        given = {name: array for name, array in arrays.items() if array is not None}
        shape = next(iter(given.values())).shape
        count = ("fresh" in given) + ("middle" in given)
        spec = pl.BlockSpec(memory_space=pltpu.VMEM)
        flags = [(name, name in given) for name in arrays]
        return pl.pallas_call(
            lambda at_end_ref, *refs: tick_body(at_end_ref, flags, *refs),
            in_specs=[pl.BlockSpec(memory_space=pltpu.SMEM)] + [spec] * len(given),
            out_specs=[spec] * count,
            out_shape=[jax.ShapeDtypeStruct(shape, LOW)] * count,
            compiler_params=pltpu.CompilerParams(vmem_limit_bytes=32 * 2**20),
            cost_estimate=QUICK,
            name="tick",
        )(self.ends, *given.values())

    def move(self, later=None):
        fresh, middle, outgoing, incoming = self.state
        if not self.on_line:
            if fresh is not None:
                total = lax.psum(fresh, "ctx")
                self.results.append((total, total))
            self.state = (later, None, None, None)
            return
        inward, outward = [(0, 1), (3, 2)], [(1, 0), (2, 3)]
        from_end = other = None
        if outgoing is not None and outgoing is incoming:
            from_end = from_middle = lax.ppermute(outgoing, "ctx", inward + outward)
        else:
            if fresh is not None:
                from_end = lax.ppermute(incoming, "ctx", inward)
            if outgoing is not None:
                from_middle = lax.ppermute(outgoing, "ctx", outward)
        if outgoing is not None:
            self.results.append((from_middle, outgoing))
        if middle is not None:
            other = lax.ppermute(middle, "ctx", [(1, 2), (2, 1)])
        pair_sum = total = None
        joined = middle is not None and later is not None and later.shape == middle.shape
        alike = fresh is None or middle is None or fresh.shape == middle.shape
        chosen = later if joined else None
        if alike and (fresh is not None or middle is not None):
            made = self.combine(
                fresh=fresh, from_end=from_end, middle=middle, other=other, later=chosen
            )
            pair_sum = made[0] if fresh is not None else None
            total = made[-1] if middle is not None else None
        elif fresh is not None:
            (pair_sum,) = self.combine(fresh=fresh, from_end=from_end)
            (total,) = self.combine(middle=middle, other=other, later=chosen)
        self.state = (later, pair_sum, total, total if joined else later)

    def fence(self, *values):
        fresh, middle, outgoing, incoming = self.state
        joined = outgoing is not None and outgoing is incoming
        held = (fresh, middle, outgoing, None if joined or incoming is fresh else incoming)
        made = self.results[self.fenced :]
        held, made, values = lax.optimization_barrier((held, made, values))
        self.results[self.fenced :] = made
        self.fenced = len(self.results)
        incoming = held[2] if joined else held[0]
        self.state = (held[0], held[1], held[2], incoming)
        return values


def attend_kernel(query_ref, key_ref, value_t_ref, mask_ref, out_ref, total_ref):
    scores = product_nt(key_ref[...], query_ref[...]) * (SCALING * LOG2E) + mask_ref[...]
    largest = jnp.max(scores, axis=0, keepdims=True)
    weights = jnp.exp2(scores - largest)
    weight_sum = jnp.sum(weights, axis=0, keepdims=True)
    gathered = product(value_t_ref[...], weights.astype(LOW))
    out_ref[...] = (gathered / weight_sum).T.astype(LOW)
    total_ref[0] = largest + jnp.log2(weight_sum)


def attend(queries, keys, values_t, mask):
    rows, key_rows = queries.shape[0], keys.shape[0]
    whole = lambda head: (0, 0)
    by_head = lambda head: (0, head)
    return pl.pallas_call(
        attend_kernel,
        grid=(H,),
        in_specs=[
            pl.BlockSpec((rows, HD), by_head),
            pl.BlockSpec((key_rows, HD), whole),
            pl.BlockSpec((HD, key_rows), whole),
            pl.BlockSpec((key_rows, rows), whole),
        ],
        out_specs=[
            pl.BlockSpec((rows, HD), by_head),
            pl.BlockSpec((1, 1, rows), lambda head: (head, 0, 0)),
        ],
        out_shape=[
            jax.ShapeDtypeStruct((rows, H * HD), LOW),
            jax.ShapeDtypeStruct((H, 1, rows), FULL),
        ],
        compiler_params=ROOMY,
        cost_estimate=QUICK,
        name="attend",
    )(queries, keys, values_t, mask)


def attend_back_kernel(
    query_ref,
    grad_ref,
    out_ref,
    total_ref,
    key_ref,
    key_t_ref,
    value_ref,
    mask_ref,
    grad_query_ref,
    grad_key_ref,
    grad_value_ref,
):
    @pl.when(pl.program_id(0) == 0)
    def _():
        grad_key_ref[...] = jnp.zeros_like(grad_key_ref)
        grad_value_ref[...] = jnp.zeros_like(grad_value_ref)

    query, grad = query_ref[...], grad_ref[...]
    scores = product_nt(key_ref[...], query) * (SCALING * LOG2E) + mask_ref[...]
    probs = jnp.exp2(scores - total_ref[0])
    grad_probs = product_nt(value_ref[...], grad)
    delta = jnp.sum((grad.astype(FULL) * out_ref[...].astype(FULL)).T, axis=0, keepdims=True)
    grad_scores = (probs * (grad_probs - delta)).astype(LOW)
    grad_value_ref[...] += product(probs.astype(LOW), grad)
    grad_key_ref[...] += product(grad_scores, query)
    grad_query_ref[...] = (product(key_t_ref[...], grad_scores).T * SCALING).astype(LOW)


def attend_back(queries, grad_out, out, totals, keys, keys_t, values, mask):
    rows, key_rows = queries.shape[0], keys.shape[0]
    whole = lambda head: (0, 0)
    by_head = lambda head: (0, head)
    return pl.pallas_call(
        attend_back_kernel,
        grid=(H,),
        in_specs=[
            pl.BlockSpec((rows, HD), by_head),
            pl.BlockSpec((rows, HD), by_head),
            pl.BlockSpec((rows, HD), by_head),
            pl.BlockSpec((1, 1, rows), lambda head: (head, 0, 0)),
            pl.BlockSpec((key_rows, HD), whole),
            pl.BlockSpec((HD, key_rows), whole),
            pl.BlockSpec((key_rows, HD), whole),
            pl.BlockSpec((key_rows, rows), whole),
        ],
        out_specs=[
            pl.BlockSpec((rows, HD), by_head),
            pl.BlockSpec((key_rows, HD), whole),
            pl.BlockSpec((key_rows, HD), whole),
        ],
        out_shape=[
            jax.ShapeDtypeStruct((rows, H * HD), LOW),
            jax.ShapeDtypeStruct((key_rows, HD), FULL),
            jax.ShapeDtypeStruct((key_rows, HD), FULL),
        ],
        compiler_params=ROOMY,
        cost_estimate=QUICK,
        name="attend_back",
    )(queries, grad_out, out, totals, keys, keys_t, values, mask)


def normalize(values_in):
    center = values_in - jnp.mean(values_in, axis=-1, keepdims=True)
    spread = jnp.mean(center * center, axis=-1, keepdims=True)
    inverse = lax.rsqrt(spread + EPSILON)
    return center * inverse, inverse


def norm_pullback(normed, inverse, gain_vec, grad_in):
    weighted = grad_in * gain_vec
    grad_values = inverse * (
        weighted
        - jnp.mean(weighted, axis=-1, keepdims=True)
        - normed * jnp.mean(weighted * normed, axis=-1, keepdims=True)
    )
    return grad_values, jnp.sum(grad_in * normed, axis=0), jnp.sum(grad_in, axis=0)


def gelu_pair(values_in):
    root = math.sqrt(2.0 / math.pi)
    square = values_in * values_in
    turned = jnp.tanh(root * values_in * (1.0 + 0.044715 * square))
    slope = 0.5 * (1.0 + turned) + 0.5 * values_in * (1.0 - turned * turned) * root * (
        1.0 + 3.0 * 0.044715 * square
    )
    return 0.5 * values_in * (1.0 + turned), slope


def per_device(
    tokens,
    segments,
    query_weight,
    pair_weight,
    out_weight,
    query_bias,
    value_bias,
    out_bias,
    norm1_gain,
    norm1_bias,
    fc_weight,
    proj_weight,
    fc_bias,
    proj_bias,
    norm2_gain,
    norm2_bias,
    cotangent,
):
    rows, width = tokens.shape[1:]
    peers = lax.axis_size("fsdp")
    depth_share = width // peers
    ctx_count = lax.axis_size("ctx")
    ctx_index = lax.axis_index("ctx")
    members = range(peers)

    spelled = by_xor() and ctx_count == 4
    ff_share = fc_weight.shape[1] // peers
    cot_own = cotangent[0]
    vectors = [query_bias, out_bias, norm1_gain, norm1_bias, proj_bias, norm2_gain, norm2_bias]
    vectors_own = jnp.concatenate(vectors + [value_bias])
    attn_weight = jnp.concatenate([query_weight, pair_weight], axis=1)
    attn_all = gather_plain(attn_weight)
    if spelled:
        packed = gather_small(vectors_own)
        held = columns_held(exchange_blocks(columns_sent(fc_weight)))
        packed, held = lax.optimization_barrier((packed, held))
        held_parts = [held, next_plane(held)]
        attn_all, packed, held_parts, out_sent = lax.optimization_barrier(
            (attn_all, packed, held_parts, out_weight)
        )
        out_near = near_rows(out_sent)
        cot_all = gather_plain(tie(cot_own, attn_all))
    else:
        packed = lax.all_gather(vectors_own, "fsdp", axis=0)
        out_all = gather_plain(out_weight)
        cot_all = gather_plain(cot_own)
        fc_all = lax.all_to_all(fc_weight, "fsdp", 1, 0, tiled=True)
    small = [
        packed[:, i * depth_share : (i + 1) * depth_share].reshape(-1).astype(FULL)
        for i in range(len(vectors))
    ]
    query_bias_all, out_bias_all, gain1, bias1, proj_bias_all, gain2, bias2 = small
    value_bias_all = packed[:, len(vectors) * depth_share :].reshape(-1).astype(FULL)

    tok_rows = tokens[0].astype(FULL)
    normed1, inverse1 = normalize(tok_rows)
    normed_in = (normed1 * gain1 + bias1).astype(LOW)
    attn_bias = jnp.concatenate([query_bias_all, jnp.zeros((HD,), FULL), value_bias_all])
    projected = (product(normed_in, attn_all) + attn_bias).astype(LOW)
    queries, pair_own = projected[:, :width], projected[:, width:]
    reach = min(ctx_count - 1, -(-(WINDOW - 1) // rows))
    pairs = [pair_own] + [
        lax.ppermute(pair_own, "ctx", [(i, i + d) for i in range(ctx_count - d)])
        for d in range(1, reach + 1)
    ]
    if spelled:
        held_parts, pairs, out_near = lax.optimization_barrier((held_parts, pairs, out_near))
        held_parts = held_parts + [next_plane(held_parts[-1])]
        out_all = gather_rows(out_sent, out_near)
    pair_rows = jnp.concatenate(pairs, axis=0)
    seg_row = segments[0]
    query_first = ctx_index * rows
    key_pos = jnp.concatenate(
        [query_first - d * rows + jnp.arange(rows, dtype=jnp.int32) for d in range(reach + 1)]
    )
    query_pos = query_first + jnp.arange(rows, dtype=jnp.int32)
    query_seg = lax.dynamic_slice_in_dim(seg_row, query_first, rows, 0)
    key_seg = jnp.concatenate(
        [
            lax.dynamic_slice_in_dim(seg_row, jnp.maximum(query_first - d * rows, 0), rows, 0)
            for d in range(reach + 1)
        ]
    )
    allowed = (
        (key_seg[:, None] == query_seg[None, :])
        & (key_pos[:, None] <= query_pos[None, :])
        & (query_pos[None, :] - key_pos[:, None] < WINDOW)
        & (key_pos[:, None] >= 0)
    )
    mask = jnp.where(allowed, 0.0, NEGATIVE).astype(FULL)
    keys, values = pair_rows[:, :HD], pair_rows[:, HD:]
    attended, score_totals = attend(queries, keys, values.T, mask)
    middle = tok_rows + (product(attended, out_all) + out_bias_all)
    normed2, inverse2 = normalize(middle)
    normed_mid = (normed2 * gain2 + bias2).astype(LOW)

    if spelled:
        held_parts, normed_mid = lax.optimization_barrier((held_parts, normed_mid))
        held_parts = held_parts + [next_plane(held_parts[-1])]
        fc_all = columns_whole(held_parts)
        mid_all = gather_rows(normed_mid, near_rows(normed_mid))
    else:
        mid_all = gather_plain(normed_mid)
    fc_bias_own = fc_bias.astype(FULL)
    piece = ff_share // 4
    ff_args = (mid_all, fc_all, fc_bias_own, cot_all, proj_weight)
    hidden, grad_pre = feed_forward(*ff_args, 0)

    def proj_term(j):
        return matmul(hidden, cot_all, "tn", 256, 1024, j * piece, piece)

    sums = SumOverCtx(proj_term(0))
    ff_args, hidden, grad_pre = sums.fence(ff_args, hidden, grad_pre)

    mid_all, fc_all, unused, cot_all, unused = ff_args
    later = proj_term(1)
    hidden, grad_pre = feed_forward(*ff_args, 1, (hidden, grad_pre))
    sums.move(later)
    mid_all, fc_all, cot_all, hidden, grad_pre = sums.fence(
        mid_all, fc_all, cot_all, hidden, grad_pre
    )

    grad_mid_part = matmul(grad_pre, fc_all, "nt")
    sums.move(proj_term(2))
    mid_all, cot_all, hidden, grad_pre, grad_mid_part = sums.fence(
        mid_all, cot_all, hidden, grad_pre, grad_mid_part
    )

    grad_normed_mid = scatter_rows(grad_mid_part)
    fc_terms = fc_gradient(mid_all, grad_pre)
    sums.move(proj_term(3))
    hidden, grad_pre, fc_terms = sums.fence(hidden, grad_pre, fc_terms)

    share_half, group = depth_share // 2, peers // 2
    fc_first = exchange_blocks([fc_terms[k, :share_half] for k in members])
    sums.move(jnp.concatenate(fc_first[:group], axis=1))
    fc_first, fc_terms, grad_normed_mid = sums.fence(fc_first, fc_terms, grad_normed_mid)
    grad_normed_mid = grad_normed_mid.astype(FULL)

    fc_second = exchange_blocks([fc_terms[k, share_half:] for k in members])
    grad_middle_ln, grad_gain2, grad_bias2 = norm_pullback(
        normed2, inverse2, gain2, grad_normed_mid
    )
    grad_middle = cot_own.astype(FULL) + grad_middle_ln
    grad_mid_low = grad_middle.astype(LOW)
    grad_attended = product_nt(grad_mid_low, out_all).astype(LOW)
    out_term = product_tn(attended, grad_mid_low).astype(LOW)
    sums.move(jnp.concatenate(fc_first[group:], axis=1))
    fc_second, grad_middle, grad_mid_low, grad_attended, out_term = sums.fence(
        fc_second, grad_middle, grad_mid_low, grad_attended, out_term
    )

    out_share = scatter_rows(out_term)
    grad_query_low, grad_keys, grad_values = attend_back(
        queries, grad_attended, attended, score_totals, keys, keys.T, values, mask
    )
    sums.move(jnp.concatenate(fc_second[:group], axis=1))
    fc_second, grad_middle, grad_mid_low, grad_query_low, grad_keys, grad_values = sums.fence(
        fc_second, grad_middle, grad_mid_low, grad_query_low, grad_keys, grad_values
    )

    grad_pairs = jnp.concatenate([grad_keys, grad_values], axis=1)
    grad_pair = grad_pairs[:rows]
    for d in range(1, reach + 1):
        sent = grad_pairs[d * rows : (d + 1) * rows].astype(LOW)
        grad_pair = grad_pair + lax.ppermute(
            sent, "ctx", [(i + d, i) for i in range(ctx_count - d)]
        ).astype(FULL)
    pair_scaling = jnp.concatenate([jnp.full((HD,), SCALING, FULL), jnp.ones((HD,), FULL)])
    grad_pair_low = (grad_pair * pair_scaling).astype(LOW)
    grad_normed_in = matmul(grad_query_low, attn_all, "nt", 256, 512, out_type=FULL)
    fc_second, grad_middle, grad_mid_low, grad_query_low, grad_pair_low, grad_normed_in = (
        sums.fence(
            fc_second, grad_middle, grad_mid_low, grad_query_low, grad_pair_low, grad_normed_in
        )
    )

    grad_normed_in = grad_normed_in + product_nt(grad_pair_low, attn_all[:, width:])
    grad_tok_ln, grad_gain1, grad_bias1 = norm_pullback(normed1, inverse1, gain1, grad_normed_in)
    grad_tokens = (grad_middle + grad_tok_ln).astype(LOW)
    grad_projected = jnp.concatenate([grad_query_low, grad_pair_low], axis=1)
    grad_projected_bias = jnp.sum(grad_projected.astype(FULL), axis=0)
    vector_terms = [
        grad_projected_bias[:width],
        jnp.sum(grad_mid_low.astype(FULL), axis=0),
        grad_gain1,
        grad_bias1,
        jnp.sum(cot_own.astype(FULL), axis=0),
        grad_gain2,
        grad_bias2,
    ]
    by_member = jnp.concatenate(
        [term.reshape(peers, depth_share) for term in vector_terms]
        + [grad_projected_bias[width + HD :].reshape(peers, HD // peers)],
        axis=1,
    )
    used, extra_cols = by_member.shape[1], grad_projected.shape[1]
    by_member = jnp.pad(by_member, ((0, 0), (0, extra_cols - used)))
    grad_fc_bias = jnp.pad(jnp.sum(grad_pre.astype(FULL), axis=0), (0, extra_cols - ff_share))
    is_own = jnp.arange(peers)[:, None] == lax.axis_index("fsdp")
    fc_bias_rows = jnp.where(is_own, grad_fc_bias[None], 0.0)
    extra = jnp.stack([by_member, fc_bias_rows], axis=1).astype(LOW)
    extra = jnp.pad(extra, ((0, 0), (0, 14), (0, 0)))
    attn_term = attn_gradient(normed_in, grad_projected, extra)
    attn_rows = attn_term.shape[1]
    attn_term = attn_term.reshape(peers * attn_rows, extra_cols)
    sums.move(jnp.concatenate(fc_second[group:], axis=1))
    hidden, attn_term = sums.fence(hidden, attn_term)

    attn_share = scatter_rows(attn_term)
    out_part = matmul(hidden, proj_weight, "nn")
    sums.move(out_share)
    (out_part,) = sums.fence(out_part)

    grad_proj = finish(sums.ends, sums.results[:4], 1)
    attn_cut = (attn_rows + 16) // 32 * 16
    sums.move(attn_share[:attn_cut])
    grad_proj, out_part = sums.fence(grad_proj, out_part)

    out_sum = scatter_rows(out_part).astype(FULL)
    output = (middle + (out_sum + proj_bias_all)).astype(LOW)
    sums.move(attn_share[attn_cut:])
    sums.fence()
    if spelled:
        grad_fc = finish(sums.ends, sums.results[4:8], 2, group)
    sums.move()
    sums.fence()
    sums.move()
    sums.fence()
    sums.move()
    sums.fence()
    if not spelled:
        grad_fc = finish(sums.ends, sums.results[4:8], 2, group)
    grad_out, attn_first, attn_second = [
        jnp.where(sums.ends[0] == 1, at_end, inside).astype(FULL)
        for at_end, inside in sums.results[8:]
    ]
    attn_sums = jnp.concatenate([attn_first, attn_second], axis=0)
    vector_sum, grad_fc_bias = attn_sums[depth_share], attn_sums[depth_share + 1, :ff_share]
    shares = [vector_sum[i * depth_share : (i + 1) * depth_share] for i in range(len(vectors))]
    value_share = vector_sum[len(vectors) * depth_share : used]
    return (
        output[None],
        grad_tokens[None],
        attn_sums[:depth_share, :width],
        attn_sums[:depth_share, width:],
        grad_out,
        shares[0],
        value_share,
        shares[1],
        shares[2],
        shares[3],
        grad_fc,
        grad_proj,
        grad_fc_bias,
        shares[4],
        shares[5],
        shares[6],
    )


def solution(mesh):
    weight, vector, token = P("fsdp", None), P("fsdp"), P("fsdp", "ctx", None)
    return jax.shard_map(
        per_device,
        mesh=mesh,
        in_specs=(
            token,
            weight,
            weight,
            weight,
            weight,
            vector,
            vector,
            vector,
            vector,
            vector,
            weight,
            weight,
            vector,
            vector,
            vector,
            vector,
            token,
        ),
        out_specs=(
            token,
            token,
            weight,
            weight,
            weight,
            vector,
            vector,
            vector,
            vector,
            vector,
            weight,
            weight,
            vector,
            vector,
            vector,
            vector,
        ),
        check_vma=False,
    )
```

```python
import math

import jax
import jax.numpy as jnp
from jax import lax
from jax.experimental import pallas as pl
from jax.experimental.pallas import tpu as pltpu
from jax.sharding import PartitionSpec as P

H = 16
HD = 128
WINDOW = 1024
EPSILON = 1e-05
NEGATIVE = -1e30
SCALING = 1.0 / math.sqrt(HD)
LOG2E = math.log2(math.e)
LOW = jnp.bfloat16
FULL = jnp.float32


def tie(value, *after):
    return lax.optimization_barrier((value, after))[0]


def product(left_side, right_side):
    return jnp.dot(left_side, right_side, preferred_element_type=FULL)


def product_tn(left_side, right_side):
    return lax.dot_general(
        left_side, right_side, (((0,), (0,)), ((), ())), preferred_element_type=FULL
    )


def product_nt(left_side, right_side):
    return lax.dot_general(
        left_side, right_side, (((1,), (1,)), ((), ())), preferred_element_type=FULL
    )


QUICK = pl.CostEstimate(flops=0, bytes_accessed=0, transcendentals=0)
ROOMY = pltpu.CompilerParams(vmem_limit_bytes=56 * 2**20)


def matmul(
    left_side,
    right_side,
    kind,
    step_rows=512,
    step_cols=2048,
    first=0,
    count=None,
    out_type=LOW,
):
    rows = count or (left_side.shape[1] if kind == "tn" else left_side.shape[0])
    depth = left_side.shape[0] if kind == "tn" else left_side.shape[1]
    cols = right_side.shape[0] if kind == "nt" else right_side.shape[1]
    step_rows, step_cols = math.gcd(step_rows, rows), math.gcd(step_cols, cols)
    inner = {"nn": product, "nt": product_nt, "tn": product_tn}[kind]
    at = first // step_rows

    def body(left_ref, right_ref, out_ref):
        out_ref[...] = inner(left_ref[...], right_ref[...]).astype(out_type)

    left_spec = (
        pl.BlockSpec((depth, step_rows), lambda j, i: (0, at + i))
        if kind == "tn"
        else pl.BlockSpec((step_rows, depth), lambda j, i: (at + i, 0))
    )
    right_spec = (
        pl.BlockSpec((step_cols, depth), lambda j, i: (j, 0))
        if kind == "nt"
        else pl.BlockSpec((depth, step_cols), lambda j, i: (0, j))
    )
    return pl.pallas_call(
        body,
        grid=(cols // step_cols, rows // step_rows),
        in_specs=[left_spec, right_spec],
        out_specs=pl.BlockSpec((step_rows, step_cols), lambda j, i: (i, j)),
        out_shape=jax.ShapeDtypeStruct((rows, cols), out_type),
        compiler_params=ROOMY,
        cost_estimate=QUICK,
        name="matmul_" + kind,
    )(left_side, right_side)


def member_order():
    return jnp.stack([member_of(k) for k in range(lax.axis_size("fsdp"))]).astype(jnp.int32)


def fc_gradient(mid_all, grad_pre):
    peers = lax.axis_size("fsdp")
    rows, width = mid_all.shape
    step, cols = width // peers, grad_pre.shape[1]

    def body(order_ref, mid_ref, grad_ref, out_ref):
        out_ref[0] = product_tn(mid_ref[...], grad_ref[...]).astype(LOW)

    return pl.pallas_call(
        body,
        grid_spec=pltpu.PrefetchScalarGridSpec(
            num_scalar_prefetch=1,
            grid=(peers,),
            in_specs=[
                pl.BlockSpec((rows, step), lambda k, order: (0, order[k])),
                pl.BlockSpec((rows, cols), lambda k, order: (0, 0)),
            ],
            out_specs=pl.BlockSpec((1, step, cols), lambda k, order: (k, 0, 0)),
        ),
        out_shape=jax.ShapeDtypeStruct((peers, step, cols), LOW),
        compiler_params=ROOMY,
        cost_estimate=QUICK,
        name="fc_gradient",
    )(member_order(), mid_all, grad_pre)


def attn_gradient(normed_in, grad_projected, extra):
    peers = lax.axis_size("fsdp")
    rows, width = normed_in.shape
    step, cols, more = width // peers, grad_projected.shape[1], extra.shape[1]

    def body(normed_ref, grad_ref, extra_ref, out_ref):
        out_ref[0, :step] = product_tn(normed_ref[...], grad_ref[...]).astype(LOW)
        out_ref[0, step:] = extra_ref[0]

    return pl.pallas_call(
        body,
        grid=(peers,),
        in_specs=[
            pl.BlockSpec((rows, step), lambda k: (0, k)),
            pl.BlockSpec((rows, cols), lambda k: (0, 0)),
            pl.BlockSpec((1, more, cols), lambda k: (k, 0, 0)),
        ],
        out_specs=pl.BlockSpec((1, step + more, cols), lambda k: (k, 0, 0)),
        out_shape=jax.ShapeDtypeStruct((peers, step + more, cols), LOW),
        compiler_params=ROOMY,
        cost_estimate=QUICK,
        name="attn_gradient",
    )(normed_in, grad_projected, extra)


def finish(ends, pairs, across, parts=1):
    rows, cols = pairs[0][0].shape
    step = cols // parts

    def body(ends_ref, order_ref, *refs):
        for c in range(len(pairs)):
            @pl.when(pl.program_id(0) == c)
            def _():
                for j in range(parts):
                    at = (slice(None), slice(j * step, (j + 1) * step))
                    chosen = jnp.where(ends_ref[0] == 1, refs[2 * c][at], refs[2 * c + 1][at])
                    place = j
                    if parts > 1:
                        place = lax.rem(order_ref[(c % across) * parts + j], parts)
                    start = pl.multiple_of(place * step, step)
                    refs[-1][:, pl.ds(start, step)] = chosen.astype(FULL)

    def placed(c, ends, order):
        row, at = c // across, lax.rem(c, across)
        return (row, order[at * parts] // parts if parts > 1 else at)

    whole = pl.BlockSpec((rows, cols), lambda c, ends, order: (0, 0))
    return pl.pallas_call(
        body,
        grid_spec=pltpu.PrefetchScalarGridSpec(
            num_scalar_prefetch=2,
            grid=(len(pairs),),
            in_specs=[whole] * (2 * len(pairs)),
            out_specs=pl.BlockSpec((rows, cols), placed),
        ),
        out_shape=jax.ShapeDtypeStruct((rows * len(pairs) // across, cols * across), FULL),
        compiler_params=ROOMY,
        cost_estimate=QUICK,
        name="finish",
    )(ends, member_order(), *[array for pair in pairs for array in pair])


def feed_forward_body(mid_ref, fc_ref, bias_ref, cot_ref, proj_ref, hidden_ref, grad_ref):
    hidden_act, slope = gelu_pair(product(mid_ref[...], fc_ref[...]) + bias_ref[...])
    hidden_ref[...] = hidden_act.astype(LOW)
    grad_ref[...] = (product_nt(cot_ref[...], proj_ref[...]) * slope).astype(LOW)


def feed_forward(mid_all, fc_all, bias, cot_all, proj, part, made=None):
    rows, width = mid_all.shape
    cols = fc_all.shape[1]
    step_rows, step = math.gcd(512, rows), cols // 2
    by_row = pl.BlockSpec((step_rows, width), lambda i: (i, 0))
    placed = pl.BlockSpec((step_rows, step), lambda i: (i, part))
    held = [] if made is None else list(made)

    def body(*refs):
        feed_forward_body(*refs[:5], *refs[-2:])

    return pl.pallas_call(
        body,
        grid=(rows // step_rows,),
        in_specs=[
            by_row,
            pl.BlockSpec((width, step), lambda i: (0, part)),
            pl.BlockSpec((1, step), lambda i: (0, part)),
            by_row,
            pl.BlockSpec((step, width), lambda i: (part, 0)),
        ]
        + [pl.BlockSpec(memory_space=pl.ANY)] * len(held),
        out_specs=[placed, placed],
        out_shape=[jax.ShapeDtypeStruct((rows, cols), LOW)] * 2,
        input_output_aliases={5: 0, 6: 1} if held else {},
        compiler_params=ROOMY,
        cost_estimate=QUICK,
        name="feed_forward",
    )(mid_all, fc_all, bias[None], cot_all, proj, *held)


def by_xor():
    return lax.axis_size("fsdp") == 8


def swap(array, bits):
    return lax.ppermute(array, "fsdp", [(i, i ^ bits) for i in range(8)])


def member_of(k):
    return lax.axis_index("fsdp") ^ k if by_xor() else jnp.int32(k)


def near_rows(own):
    return swap(own, 2), swap(own, 4)


def placed_own(own):
    def body(order_ref, own_ref, out_ref):
        out_ref[...] = own_ref[...]

    return pl.pallas_call(
        body,
        grid_spec=pltpu.PrefetchScalarGridSpec(
            num_scalar_prefetch=1,
            grid=(1,),
            in_specs=[pl.BlockSpec(own.shape, lambda k, order: (0, 0))],
            out_specs=pl.BlockSpec(own.shape, lambda k, order: (order[0], 0)),
        ),
        out_shape=jax.ShapeDtypeStruct((8 * own.shape[0], own.shape[1]), own.dtype),
        compiler_params=ROOMY,
        cost_estimate=QUICK,
        name="placed_own",
    )(member_order(), own)


def gather_rows(own, near):
    count = own.shape[0]
    half = count // 2
    near, whole = lax.optimization_barrier((near, placed_own(own)))
    along_x, along_y = near
    first_half, second_half = swap(along_x[:half], 4), swap(along_y[half:], 2)
    placed = [
        (1, 0, swap(own, 1)),
        (2, 0, along_x),
        (4, 0, along_y),
        (3, 0, swap(along_x, 1)),
        (5, 0, swap(along_y, 1)),
        (6, 0, first_half),
        (6, half, second_half),
        (7, 0, swap(first_half, 1)),
        (7, half, swap(second_half, 1)),
    ]
    for k, offset, block in placed:
        whole = lax.dynamic_update_slice(whole, block, (member_of(k) * count + offset, 0))
    return whole


def gather_plain(own):
    return lax.all_gather(own, "fsdp", axis=0, tiled=True)


def gather_small(own):
    held = own[None]
    for bits in (1, 2, 4):
        held = jnp.concatenate([held, swap(held, bits)], axis=0)
    return relative(held, 0)


def scatter_rows(array):
    return lax.psum_scatter(array, "fsdp", scatter_dimension=0, tiled=True)


def exchange_blocks(blocks):
    if not by_xor():
        moved = lax.all_to_all(jnp.stack(blocks), "fsdp", 0, 0, tiled=True)
        return [moved[k] for k in range(len(blocks))]
    moved = {0: blocks[0]}
    for k in (2, 4, 6, 1, 3, 5, 7):
        moved[k] = swap(blocks[k], k)
    return [moved[k] for k in range(8)]


def relative(array, axis):
    if not by_xor():
        return array
    step = array.shape[axis] // 8
    return jnp.concatenate(
        [lax.dynamic_slice_in_dim(array, member_of(k) * step, step, axis) for k in range(8)],
        axis=axis,
    )


def columns_sent(own):
    planes = lax.axis_size("ctx")
    part, share = own.shape[0] // planes, own.shape[1] // 8
    place = lax.axis_index("ctx")
    return [
        lax.dynamic_slice(own, (place * part, member_of(k) * share), (part, share)) for k in range(8)
    ]


def columns_held(moved):
    held = jnp.zeros((8,) + moved[0].shape, moved[0].dtype)
    for k in range(8):
        held = lax.dynamic_update_slice(held, moved[k][None], (member_of(k), 0, 0))
    return held


def next_plane(held):
    planes = lax.axis_size("ctx")
    return lax.ppermute(held, "ctx", [(i, (i + 1) % planes) for i in range(planes)])


def columns_whole(held_parts):
    planes = len(held_parts)
    peers, part, share = held_parts[0].shape
    whole = jnp.zeros((peers, planes, part, share), held_parts[0].dtype)
    for step, held in enumerate(held_parts):
        source = lax.rem(lax.axis_index("ctx") + planes - step, planes)
        whole = lax.dynamic_update_slice(whole, held[:, None], (0, source, 0, 0))
    return whole.reshape(peers * planes * part, share)


def tick_body(at_end_ref, given, *refs):
    names = [name for name, there in given if there]
    held = dict(zip(names, refs))
    made = list(refs[len(names) :])

    def add(first, second):
        return (held[first][...].astype(FULL) + held[second][...].astype(FULL)).astype(LOW)

    if "fresh" in held:
        made.pop(0)[...] = add("fresh", "from_end")
    if "middle" in held:
        total = add("middle", "other")
        if "later" in held:
            total = jnp.where(at_end_ref[0] == 1, held["later"][...], total)
        made.pop(0)[...] = total


class SumOverCtx:
    def __init__(self, first):
        self.on_line = lax.axis_size("ctx") == 4
        place = lax.axis_index("ctx")
        self.ends = ((place == 0) | (place == 3)).astype(jnp.int32)[None]
        self.state = (first, None, None, first)
        self.results = []
        self.fenced = 0

    def combine(self, **arrays):
        given = {name: array for name, array in arrays.items() if array is not None}
        shape = next(iter(given.values())).shape
        count = ("fresh" in given) + ("middle" in given)
        spec = pl.BlockSpec(memory_space=pltpu.VMEM)
        flags = [(name, name in given) for name in arrays]
        return pl.pallas_call(
            lambda at_end_ref, *refs: tick_body(at_end_ref, flags, *refs),
            in_specs=[pl.BlockSpec(memory_space=pltpu.SMEM)] + [spec] * len(given),
            out_specs=[spec] * count,
            out_shape=[jax.ShapeDtypeStruct(shape, LOW)] * count,
            compiler_params=pltpu.CompilerParams(vmem_limit_bytes=32 * 2**20),
            cost_estimate=QUICK,
            name="tick",
        )(self.ends, *given.values())

    def move(self, later=None):
        fresh, middle, outgoing, incoming = self.state
        if not self.on_line:
            if fresh is not None:
                total = lax.psum(fresh, "ctx")
                self.results.append((total, total))
            self.state = (later, None, None, None)
            return
        inward, outward = [(0, 1), (3, 2)], [(1, 0), (2, 3)]
        from_end = other = None
        if outgoing is not None and outgoing is incoming:
            from_end = from_middle = lax.ppermute(outgoing, "ctx", inward + outward)
        else:
            if fresh is not None:
                from_end = lax.ppermute(incoming, "ctx", inward)
            if outgoing is not None:
                from_middle = lax.ppermute(outgoing, "ctx", outward)
        if outgoing is not None:
            self.results.append((from_middle, outgoing))
        if middle is not None:
            other = lax.ppermute(middle, "ctx", [(1, 2), (2, 1)])
        pair_sum = total = None
        joined = middle is not None and later is not None and later.shape == middle.shape
        alike = fresh is None or middle is None or fresh.shape == middle.shape
        chosen = later if joined else None
        if alike and (fresh is not None or middle is not None):
            made = self.combine(
                fresh=fresh, from_end=from_end, middle=middle, other=other, later=chosen
            )
            pair_sum = made[0] if fresh is not None else None
            total = made[-1] if middle is not None else None
        elif fresh is not None:
            (pair_sum,) = self.combine(fresh=fresh, from_end=from_end)
            (total,) = self.combine(middle=middle, other=other, later=chosen)
        self.state = (later, pair_sum, total, total if joined else later)

    def fence(self, *values):
        fresh, middle, outgoing, incoming = self.state
        joined = outgoing is not None and outgoing is incoming
        held = (fresh, middle, outgoing, None if joined or incoming is fresh else incoming)
        made = self.results[self.fenced :]
        held, made, values = lax.optimization_barrier((held, made, values))
        self.results[self.fenced :] = made
        self.fenced = len(self.results)
        incoming = held[2] if joined else held[0]
        self.state = (held[0], held[1], held[2], incoming)
        return values


def attend_kernel(query_ref, key_ref, value_t_ref, mask_ref, out_ref, total_ref):
    scores = product_nt(key_ref[...], query_ref[...]) * (SCALING * LOG2E) + mask_ref[...]
    largest = jnp.max(scores, axis=0, keepdims=True)
    weights = jnp.exp2(scores - largest)
    weight_sum = jnp.sum(weights, axis=0, keepdims=True)
    gathered = product(value_t_ref[...], weights.astype(LOW))
    out_ref[...] = (gathered / weight_sum).T.astype(LOW)
    total_ref[0] = largest + jnp.log2(weight_sum)


def attend(queries, keys, values_t, mask):
    rows, key_rows = queries.shape[0], keys.shape[0]
    whole = lambda head: (0, 0)
    by_head = lambda head: (0, head)
    return pl.pallas_call(
        attend_kernel,
        grid=(H,),
        in_specs=[
            pl.BlockSpec((rows, HD), by_head),
            pl.BlockSpec((key_rows, HD), whole),
            pl.BlockSpec((HD, key_rows), whole),
            pl.BlockSpec((key_rows, rows), whole),
        ],
        out_specs=[
            pl.BlockSpec((rows, HD), by_head),
            pl.BlockSpec((1, 1, rows), lambda head: (head, 0, 0)),
        ],
        out_shape=[
            jax.ShapeDtypeStruct((rows, H * HD), LOW),
            jax.ShapeDtypeStruct((H, 1, rows), FULL),
        ],
        compiler_params=ROOMY,
        cost_estimate=QUICK,
        name="attend",
    )(queries, keys, values_t, mask)


def attend_back_kernel(
    query_ref,
    grad_ref,
    out_ref,
    total_ref,
    key_ref,
    key_t_ref,
    value_ref,
    mask_ref,
    grad_query_ref,
    grad_key_ref,
    grad_value_ref,
):
    @pl.when(pl.program_id(0) == 0)
    def _():
        grad_key_ref[...] = jnp.zeros_like(grad_key_ref)
        grad_value_ref[...] = jnp.zeros_like(grad_value_ref)

    query, grad = query_ref[...], grad_ref[...]
    scores = product_nt(key_ref[...], query) * (SCALING * LOG2E) + mask_ref[...]
    probs = jnp.exp2(scores - total_ref[0])
    grad_probs = product_nt(value_ref[...], grad)
    delta = jnp.sum((grad.astype(FULL) * out_ref[...].astype(FULL)).T, axis=0, keepdims=True)
    grad_scores = (probs * (grad_probs - delta)).astype(LOW)
    grad_value_ref[...] += product(probs.astype(LOW), grad)
    grad_key_ref[...] += product(grad_scores, query)
    grad_query_ref[...] = (product(key_t_ref[...], grad_scores).T * SCALING).astype(LOW)


def attend_back(queries, grad_out, out, totals, keys, keys_t, values, mask):
    rows, key_rows = queries.shape[0], keys.shape[0]
    whole = lambda head: (0, 0)
    by_head = lambda head: (0, head)
    return pl.pallas_call(
        attend_back_kernel,
        grid=(H,),
        in_specs=[
            pl.BlockSpec((rows, HD), by_head),
            pl.BlockSpec((rows, HD), by_head),
            pl.BlockSpec((rows, HD), by_head),
            pl.BlockSpec((1, 1, rows), lambda head: (head, 0, 0)),
            pl.BlockSpec((key_rows, HD), whole),
            pl.BlockSpec((HD, key_rows), whole),
            pl.BlockSpec((key_rows, HD), whole),
            pl.BlockSpec((key_rows, rows), whole),
        ],
        out_specs=[
            pl.BlockSpec((rows, HD), by_head),
            pl.BlockSpec((key_rows, HD), whole),
            pl.BlockSpec((key_rows, HD), whole),
        ],
        out_shape=[
            jax.ShapeDtypeStruct((rows, H * HD), LOW),
            jax.ShapeDtypeStruct((key_rows, HD), FULL),
            jax.ShapeDtypeStruct((key_rows, HD), FULL),
        ],
        compiler_params=ROOMY,
        cost_estimate=QUICK,
        name="attend_back",
    )(queries, grad_out, out, totals, keys, keys_t, values, mask)


def normalize(values_in):
    center = values_in - jnp.mean(values_in, axis=-1, keepdims=True)
    spread = jnp.mean(center * center, axis=-1, keepdims=True)
    inverse = lax.rsqrt(spread + EPSILON)
    return center * inverse, inverse


def norm_pullback(normed, inverse, gain, grad_in, base, pair=None, weight=None, out_type=FULL):
    rows, width = normed.shape
    more = [] if pair is None else [pair, weight]

    def body(normed_ref, inverse_ref, gain_ref, grad_ref, base_ref, *refs):
        out_ref, sums_ref = refs[-2:]
        grad = grad_ref[...].astype(FULL)
        if more:
            grad = grad + product_nt(refs[0][...], refs[1][...])
        held = normed_ref[...]
        weighted = grad * gain_ref[...]
        turned = inverse_ref[...] * (
            weighted
            - jnp.mean(weighted, axis=-1, keepdims=True)
            - held * jnp.mean(weighted * held, axis=-1, keepdims=True)
        )
        made = base_ref[...].astype(FULL) + turned
        out_ref[...] = made.astype(out_type)
        sums_ref[0:1] = jnp.sum(grad * held, axis=0, keepdims=True)
        sums_ref[1:2] = jnp.sum(grad, axis=0, keepdims=True)
        sums_ref[2:3] = jnp.sum(made.astype(LOW).astype(FULL), axis=0, keepdims=True)

    at = lambda i: (0, 0)
    specs = [pl.BlockSpec(array.shape, at) for array in (normed, inverse, gain[None], grad_in, base)]
    if more:
        cols = pair.shape[1]
        last = weight.shape[1] // cols - 1
        specs += [pl.BlockSpec(pair.shape, at), pl.BlockSpec((width, cols), lambda i: (0, last))]
    made, sums = pl.pallas_call(
        body,
        grid=(1,),
        in_specs=specs,
        out_specs=[pl.BlockSpec((rows, width), at), pl.BlockSpec((8, width), at)],
        out_shape=[
            jax.ShapeDtypeStruct((rows, width), out_type),
            jax.ShapeDtypeStruct((8, width), FULL),
        ],
        compiler_params=ROOMY,
        cost_estimate=QUICK,
        name="norm_pullback",
    )(normed, inverse, gain[None], grad_in, base, *more)
    return made, sums[0], sums[1], sums[2]


def gelu_pair(values_in):
    root = math.sqrt(2.0 / math.pi)
    square = values_in * values_in
    turned = jnp.tanh(root * values_in * (1.0 + 0.044715 * square))
    slope = 0.5 * (1.0 + turned) + 0.5 * values_in * (1.0 - turned * turned) * root * (
        1.0 + 3.0 * 0.044715 * square
    )
    return 0.5 * values_in * (1.0 + turned), slope


def per_device(
    tokens,
    segments,
    query_weight,
    pair_weight,
    out_weight,
    query_bias,
    value_bias,
    out_bias,
    norm1_gain,
    norm1_bias,
    fc_weight,
    proj_weight,
    fc_bias,
    proj_bias,
    norm2_gain,
    norm2_bias,
    cotangent,
):
    rows, width = tokens.shape[1:]
    peers = lax.axis_size("fsdp")
    depth_share = width // peers
    ctx_count = lax.axis_size("ctx")
    ctx_index = lax.axis_index("ctx")
    members = range(peers)

    spelled = by_xor() and ctx_count == 4
    ff_share = fc_weight.shape[1] // peers
    cot_own = cotangent[0]
    vectors = [query_bias, out_bias, norm1_gain, norm1_bias, proj_bias, norm2_gain, norm2_bias]
    vectors_own = jnp.concatenate(vectors + [value_bias])
    attn_weight = jnp.concatenate([query_weight, pair_weight], axis=1)
    attn_all = gather_plain(attn_weight)
    if spelled:
        packed = gather_small(vectors_own)
        held = columns_held(exchange_blocks(columns_sent(fc_weight)))
        packed, held = lax.optimization_barrier((packed, held))
        held_parts = [held, next_plane(held)]
        attn_all, packed, held_parts, out_sent = lax.optimization_barrier(
            (attn_all, packed, held_parts, out_weight)
        )
        out_near = near_rows(out_sent)
        cot_all = gather_plain(tie(cot_own, attn_all))
    else:
        packed = lax.all_gather(vectors_own, "fsdp", axis=0)
        out_all = gather_plain(out_weight)
        cot_all = gather_plain(cot_own)
        fc_all = lax.all_to_all(fc_weight, "fsdp", 1, 0, tiled=True)
    small = [
        packed[:, i * depth_share : (i + 1) * depth_share].reshape(-1).astype(FULL)
        for i in range(len(vectors))
    ]
    query_bias_all, out_bias_all, gain1, bias1, proj_bias_all, gain2, bias2 = small
    value_bias_all = packed[:, len(vectors) * depth_share :].reshape(-1).astype(FULL)

    tok_rows = tokens[0].astype(FULL)
    normed1, inverse1 = normalize(tok_rows)
    normed_in = (normed1 * gain1 + bias1).astype(LOW)
    attn_bias = jnp.concatenate([query_bias_all, jnp.zeros((HD,), FULL), value_bias_all])
    projected = (product(normed_in, attn_all) + attn_bias).astype(LOW)
    pair_own = projected[:, width:]
    reach = min(ctx_count - 1, -(-(WINDOW - 1) // rows))
    pairs = [pair_own] + [
        lax.ppermute(pair_own, "ctx", [(i, i + d) for i in range(ctx_count - d)])
        for d in range(1, reach + 1)
    ]
    if spelled:
        held_parts, pairs, out_near = lax.optimization_barrier((held_parts, pairs, out_near))
        held_parts = held_parts + [next_plane(held_parts[-1])]
        out_all = gather_rows(out_sent, out_near)
    pair_rows = jnp.concatenate(pairs, axis=0)
    seg_row = segments[0]
    query_first = ctx_index * rows
    key_pos = jnp.concatenate(
        [query_first - d * rows + jnp.arange(rows, dtype=jnp.int32) for d in range(reach + 1)]
    )
    query_pos = query_first + jnp.arange(rows, dtype=jnp.int32)
    query_seg = lax.dynamic_slice_in_dim(seg_row, query_first, rows, 0)
    key_seg = jnp.concatenate(
        [
            lax.dynamic_slice_in_dim(seg_row, jnp.maximum(query_first - d * rows, 0), rows, 0)
            for d in range(reach + 1)
        ]
    )
    allowed = (
        (key_seg[:, None] == query_seg[None, :])
        & (key_pos[:, None] <= query_pos[None, :])
        & (query_pos[None, :] - key_pos[:, None] < WINDOW)
        & (key_pos[:, None] >= 0)
    )
    mask = jnp.where(allowed, 0.0, NEGATIVE).astype(FULL)
    keys, values = pair_rows[:, :HD], pair_rows[:, HD:]
    attended, score_totals = attend(projected, keys, values.T, mask)
    middle = tok_rows + (product(attended, out_all) + out_bias_all)
    normed2, inverse2 = normalize(middle)
    normed_mid = (normed2 * gain2 + bias2).astype(LOW)

    if spelled:
        held_parts, normed_mid = lax.optimization_barrier((held_parts, normed_mid))
        held_parts = held_parts + [next_plane(held_parts[-1])]
        fc_all = columns_whole(held_parts)
        mid_all = gather_rows(normed_mid, near_rows(normed_mid))
    else:
        mid_all = gather_plain(normed_mid)
    fc_bias_own = fc_bias.astype(FULL)
    piece = ff_share // 4
    ff_args = (mid_all, fc_all, fc_bias_own, cot_all, proj_weight)
    hidden, grad_pre = feed_forward(*ff_args, 0)

    def proj_term(j):
        return matmul(hidden, cot_all, "tn", 256, 1024, j * piece, piece)

    sums = SumOverCtx(proj_term(0))
    ff_args, hidden, grad_pre = sums.fence(ff_args, hidden, grad_pre)

    mid_all, fc_all, unused, cot_all, unused = ff_args
    later = proj_term(1)
    hidden, grad_pre = feed_forward(*ff_args, 1, (hidden, grad_pre))
    sums.move(later)
    mid_all, fc_all, cot_all, hidden, grad_pre = sums.fence(
        mid_all, fc_all, cot_all, hidden, grad_pre
    )

    grad_mid_part = matmul(grad_pre, fc_all, "nt")
    grad_normed_mid = scatter_rows(grad_mid_part)
    fc_terms = fc_gradient(mid_all, grad_pre)
    sums.move(proj_term(2))
    cot_all, hidden, grad_pre, grad_mid_part, fc_terms = sums.fence(
        cot_all, hidden, grad_pre, grad_mid_part, fc_terms
    )

    share_half, group = depth_share // 2, peers // 2
    fc_first = exchange_blocks([fc_terms[k, :share_half] for k in members])
    grad_fc_bias = jnp.sum(grad_pre.astype(FULL), axis=0)
    cot_sum = jnp.sum(cot_own.astype(FULL), axis=0)
    sums.move(proj_term(3))
    hidden, fc_terms, fc_first, grad_fc_bias, cot_sum = sums.fence(
        hidden, fc_terms, fc_first, grad_fc_bias, cot_sum
    )

    fc_second = exchange_blocks([fc_terms[k, share_half:] for k in members])
    sums.move(jnp.concatenate(fc_first[:group], axis=1))
    fc_first, fc_second, grad_normed_mid = sums.fence(fc_first, fc_second, grad_normed_mid)

    grad_middle, grad_gain2, grad_bias2, grad_mid_sum = norm_pullback(
        normed2, inverse2, gain2, grad_normed_mid, cot_own
    )
    grad_mid_low = grad_middle.astype(LOW)
    grad_attended = matmul(grad_mid_low, out_all, "nt", 256, 512)
    out_term = matmul(attended, grad_mid_low, "tn", 512, 2048)
    sums.move(jnp.concatenate(fc_first[group:], axis=1))
    fc_second, grad_middle, grad_attended, out_term, grad_mid_sum = sums.fence(
        fc_second, grad_middle, grad_attended, out_term, grad_mid_sum
    )

    out_share = scatter_rows(out_term)
    grad_query_low, grad_keys, grad_values = attend_back(
        projected, grad_attended, attended, score_totals, keys, keys.T, values, mask
    )
    sums.move(jnp.concatenate(fc_second[:group], axis=1))
    fc_second, grad_query_low, grad_keys, grad_values = sums.fence(
        fc_second, grad_query_low, grad_keys, grad_values
    )

    grad_pairs = jnp.concatenate([grad_keys, grad_values], axis=1)
    grad_pair = grad_pairs[:rows]
    for d in range(1, reach + 1):
        sent = grad_pairs[d * rows : (d + 1) * rows].astype(LOW)
        grad_pair = grad_pair + lax.ppermute(
            sent, "ctx", [(i + d, i) for i in range(ctx_count - d)]
        ).astype(FULL)
    pair_scaling = jnp.concatenate([jnp.full((HD,), SCALING, FULL), jnp.ones((HD,), FULL)])
    grad_pair_low = (grad_pair * pair_scaling).astype(LOW)
    grad_normed_in = matmul(grad_query_low, attn_all, "nt", 256, 512, out_type=FULL)
    query_sum = jnp.sum(grad_query_low.astype(FULL), axis=0)
    fc_second, grad_query_low, grad_pair_low, grad_normed_in, query_sum = sums.fence(
        fc_second, grad_query_low, grad_pair_low, grad_normed_in, query_sum
    )

    grad_tokens, grad_gain1, grad_bias1, unused = norm_pullback(
        normed1,
        inverse1,
        gain1,
        grad_normed_in,
        grad_middle,
        grad_pair_low,
        attn_all,
        LOW,
    )
    grad_projected = jnp.concatenate([grad_query_low, grad_pair_low], axis=1)
    pair_sum = jnp.sum(grad_pair_low.astype(FULL), axis=0)
    vector_terms = [
        query_sum,
        grad_mid_sum,
        grad_gain1,
        grad_bias1,
        cot_sum,
        grad_gain2,
        grad_bias2,
    ]
    by_member = jnp.concatenate(
        [term.reshape(peers, depth_share) for term in vector_terms]
        + [pair_sum[HD:].reshape(peers, HD // peers)],
        axis=1,
    )
    used, extra_cols = by_member.shape[1], grad_projected.shape[1]
    by_member = jnp.pad(by_member, ((0, 0), (0, extra_cols - used)))
    grad_fc_bias = jnp.pad(grad_fc_bias, (0, extra_cols - ff_share))
    is_own = jnp.arange(peers)[:, None] == lax.axis_index("fsdp")
    fc_bias_rows = jnp.where(is_own, grad_fc_bias[None], 0.0)
    extra = jnp.stack([by_member, fc_bias_rows], axis=1).astype(LOW)
    extra = jnp.pad(extra, ((0, 0), (0, 14), (0, 0)))
    attn_term = attn_gradient(normed_in, grad_projected, extra)
    attn_rows = attn_term.shape[1]
    attn_term = attn_term.reshape(peers * attn_rows, extra_cols)
    attn_share = scatter_rows(attn_term)
    sums.move(jnp.concatenate(fc_second[group:], axis=1))
    hidden, attn_term = sums.fence(hidden, attn_term)

    out_part = matmul(hidden, proj_weight, "nn")
    sums.move(out_share)
    (out_part,) = sums.fence(out_part)

    grad_proj = finish(sums.ends, sums.results[:4], 1)
    attn_cut = (attn_rows + 16) // 32 * 16
    sums.move(attn_share[:attn_cut])
    grad_proj, out_part = sums.fence(grad_proj, out_part)

    out_sum = scatter_rows(out_part).astype(FULL)
    output = (middle + (out_sum + proj_bias_all)).astype(LOW)
    sums.move(attn_share[attn_cut:])
    sums.fence()
    if spelled:
        grad_fc = finish(sums.ends, sums.results[4:8], 2, group)
    sums.move()
    sums.fence()
    sums.move()
    sums.fence()
    sums.move()
    sums.fence()
    if not spelled:
        grad_fc = finish(sums.ends, sums.results[4:8], 2, group)
    grad_out, attn_first, attn_second = [
        jnp.where(sums.ends[0] == 1, at_end, inside).astype(FULL)
        for at_end, inside in sums.results[8:]
    ]
    attn_sums = jnp.concatenate([attn_first, attn_second], axis=0)
    vector_sum, grad_fc_bias = attn_sums[depth_share], attn_sums[depth_share + 1, :ff_share]
    shares = [vector_sum[i * depth_share : (i + 1) * depth_share] for i in range(len(vectors))]
    value_share = vector_sum[len(vectors) * depth_share : used]
    return (
        output[None],
        grad_tokens[None],
        attn_sums[:depth_share, :width],
        attn_sums[:depth_share, width:],
        grad_out,
        shares[0],
        value_share,
        shares[1],
        shares[2],
        shares[3],
        grad_fc,
        grad_proj,
        grad_fc_bias,
        shares[4],
        shares[5],
        shares[6],
    )


def solution(mesh):
    weight, vector, token = P("fsdp", None), P("fsdp"), P("fsdp", "ctx", None)
    return jax.shard_map(
        per_device,
        mesh=mesh,
        in_specs=(
            token,
            weight,
            weight,
            weight,
            weight,
            vector,
            vector,
            vector,
            vector,
            vector,
            weight,
            weight,
            vector,
            vector,
            vector,
            vector,
            token,
        ),
        out_specs=(
            token,
            token,
            weight,
            weight,
            weight,
            vector,
            vector,
            vector,
            vector,
            vector,
            weight,
            weight,
            vector,
            vector,
            vector,
            vector,
        ),
        check_vma=False,
    )
```

```python
import math

import jax
import jax.numpy as jnp
from jax import lax
from jax.experimental import pallas as pl
from jax.experimental.pallas import tpu as pltpu
from jax.sharding import PartitionSpec as P

H = 16
HD = 128
WINDOW = 1024
EPSILON = 1e-05
NEGATIVE = -1e30
SCALING = 1.0 / math.sqrt(HD)
LOG2E = math.log2(math.e)
LOW = jnp.bfloat16
FULL = jnp.float32


def tie(value, *after):
    return lax.optimization_barrier((value, after))[0]


def product(left_side, right_side):
    return jnp.dot(left_side, right_side, preferred_element_type=FULL)


def product_tn(left_side, right_side):
    return lax.dot_general(
        left_side, right_side, (((0,), (0,)), ((), ())), preferred_element_type=FULL
    )


def product_nt(left_side, right_side):
    return lax.dot_general(
        left_side, right_side, (((1,), (1,)), ((), ())), preferred_element_type=FULL
    )


QUICK = pl.CostEstimate(flops=0, bytes_accessed=0, transcendentals=0)
ROOMY = pltpu.CompilerParams(vmem_limit_bytes=56 * 2**20)


def matmul(
    left_side,
    right_side,
    kind,
    step_rows=512,
    step_cols=2048,
    first=0,
    count=None,
    out_type=LOW,
):
    rows = count or (left_side.shape[1] if kind == "tn" else left_side.shape[0])
    depth = left_side.shape[0] if kind == "tn" else left_side.shape[1]
    cols = right_side.shape[0] if kind == "nt" else right_side.shape[1]
    step_rows, step_cols = math.gcd(step_rows, rows), math.gcd(step_cols, cols)
    inner = {"nn": product, "nt": product_nt, "tn": product_tn}[kind]
    at = first // step_rows

    def body(left_ref, right_ref, out_ref):
        out_ref[...] = inner(left_ref[...], right_ref[...]).astype(out_type)

    left_spec = (
        pl.BlockSpec((depth, step_rows), lambda j, i: (0, at + i))
        if kind == "tn"
        else pl.BlockSpec((step_rows, depth), lambda j, i: (at + i, 0))
    )
    right_spec = (
        pl.BlockSpec((step_cols, depth), lambda j, i: (j, 0))
        if kind == "nt"
        else pl.BlockSpec((depth, step_cols), lambda j, i: (0, j))
    )
    return pl.pallas_call(
        body,
        grid=(cols // step_cols, rows // step_rows),
        in_specs=[left_spec, right_spec],
        out_specs=pl.BlockSpec((step_rows, step_cols), lambda j, i: (i, j)),
        out_shape=jax.ShapeDtypeStruct((rows, cols), out_type),
        compiler_params=ROOMY,
        cost_estimate=QUICK,
        name="matmul_" + kind,
    )(left_side, right_side)


def member_order():
    return jnp.stack([member_of(k) for k in range(lax.axis_size("fsdp"))]).astype(jnp.int32)


def fc_gradient(mid_all, grad_pre):
    peers = lax.axis_size("fsdp")
    rows, width = mid_all.shape
    step, cols = width // peers, grad_pre.shape[1]

    def body(order_ref, mid_ref, grad_ref, out_ref):
        out_ref[0] = product_tn(mid_ref[...], grad_ref[...]).astype(LOW)

    return pl.pallas_call(
        body,
        grid_spec=pltpu.PrefetchScalarGridSpec(
            num_scalar_prefetch=1,
            grid=(peers,),
            in_specs=[
                pl.BlockSpec((rows, step), lambda k, order: (0, order[k])),
                pl.BlockSpec((rows, cols), lambda k, order: (0, 0)),
            ],
            out_specs=pl.BlockSpec((1, step, cols), lambda k, order: (k, 0, 0)),
        ),
        out_shape=jax.ShapeDtypeStruct((peers, step, cols), LOW),
        compiler_params=ROOMY,
        cost_estimate=QUICK,
        name="fc_gradient",
    )(member_order(), mid_all, grad_pre)


def attn_gradient(normed_in, grad_query, grad_pair, extra):
    peers = lax.axis_size("fsdp")
    rows, width = normed_in.shape
    query_cols, pair_cols = grad_query.shape[1], grad_pair.shape[1]
    step, cols, more = width // peers, query_cols + pair_cols, extra.shape[1]

    def body(normed_ref, query_ref, pair_ref, extra_ref, out_ref):
        out_ref[0, :step, :query_cols] = product_tn(normed_ref[...], query_ref[...]).astype(LOW)
        out_ref[0, :step, query_cols:] = product_tn(normed_ref[...], pair_ref[...]).astype(LOW)
        out_ref[0, step:] = extra_ref[0]

    return pl.pallas_call(
        body,
        grid=(peers,),
        in_specs=[
            pl.BlockSpec((rows, step), lambda k: (0, k)),
            pl.BlockSpec((rows, query_cols), lambda k: (0, 0)),
            pl.BlockSpec((rows, pair_cols), lambda k: (0, 0)),
            pl.BlockSpec((1, more, cols), lambda k: (k, 0, 0)),
        ],
        out_specs=pl.BlockSpec((1, step + more, cols), lambda k: (k, 0, 0)),
        out_shape=jax.ShapeDtypeStruct((peers, step + more, cols), LOW),
        compiler_params=ROOMY,
        cost_estimate=QUICK,
        name="attn_gradient",
    )(normed_in, grad_query, grad_pair, extra)


def finish(ends, pairs, across, parts=1):
    rows, cols = pairs[0][0].shape
    step = cols // parts

    def body(ends_ref, order_ref, *refs):
        for c in range(len(pairs)):
            @pl.when(pl.program_id(0) == c)
            def _():
                for j in range(parts):
                    at = (slice(None), slice(j * step, (j + 1) * step))
                    chosen = jnp.where(ends_ref[0] == 1, refs[2 * c][at], refs[2 * c + 1][at])
                    place = j
                    if parts > 1:
                        place = lax.rem(order_ref[(c % across) * parts + j], parts)
                    start = pl.multiple_of(place * step, step)
                    refs[-1][:, pl.ds(start, step)] = chosen.astype(FULL)

    def placed(c, ends, order):
        row, at = c // across, lax.rem(c, across)
        return (row, order[at * parts] // parts if parts > 1 else at)

    whole = pl.BlockSpec((rows, cols), lambda c, ends, order: (0, 0))
    return pl.pallas_call(
        body,
        grid_spec=pltpu.PrefetchScalarGridSpec(
            num_scalar_prefetch=2,
            grid=(len(pairs),),
            in_specs=[whole] * (2 * len(pairs)),
            out_specs=pl.BlockSpec((rows, cols), placed),
        ),
        out_shape=jax.ShapeDtypeStruct((rows * len(pairs) // across, cols * across), FULL),
        compiler_params=ROOMY,
        cost_estimate=QUICK,
        name="finish",
    )(ends, member_order(), *[array for pair in pairs for array in pair])


def feed_forward_body(mid_ref, fc_ref, bias_ref, cot_ref, proj_ref, hidden_ref, grad_ref):
    hidden_act, slope = gelu_pair(product(mid_ref[...], fc_ref[...]) + bias_ref[...])
    hidden_ref[...] = hidden_act.astype(LOW)
    grad_ref[...] = (product_nt(cot_ref[...], proj_ref[...]) * slope).astype(LOW)


def feed_forward(mid_all, fc_all, bias, cot_all, proj, part, made=None):
    rows, width = mid_all.shape
    cols = fc_all.shape[1]
    step_rows, step = math.gcd(512, rows), cols // 2
    by_row = pl.BlockSpec((step_rows, width), lambda i: (i, 0))
    placed = pl.BlockSpec((step_rows, step), lambda i: (i, part))
    held = [] if made is None else list(made)

    def body(*refs):
        feed_forward_body(*refs[:5], *refs[-2:])

    return pl.pallas_call(
        body,
        grid=(rows // step_rows,),
        in_specs=[
            by_row,
            pl.BlockSpec((width, step), lambda i: (0, part)),
            pl.BlockSpec((1, step), lambda i: (0, part)),
            by_row,
            pl.BlockSpec((step, width), lambda i: (part, 0)),
        ]
        + [pl.BlockSpec(memory_space=pl.ANY)] * len(held),
        out_specs=[placed, placed],
        out_shape=[jax.ShapeDtypeStruct((rows, cols), LOW)] * 2,
        input_output_aliases={5: 0, 6: 1} if held else {},
        compiler_params=ROOMY,
        cost_estimate=QUICK,
        name="feed_forward",
    )(mid_all, fc_all, bias[None], cot_all, proj, *held)


def by_xor():
    return lax.axis_size("fsdp") == 8


def swap(array, bits):
    return lax.ppermute(array, "fsdp", [(i, i ^ bits) for i in range(8)])


def member_of(k):
    return lax.axis_index("fsdp") ^ k if by_xor() else jnp.int32(k)


def near_rows(own):
    return swap(own, 2), swap(own, 4)


def placed_own(own):
    def body(order_ref, own_ref, out_ref):
        out_ref[...] = own_ref[...]

    return pl.pallas_call(
        body,
        grid_spec=pltpu.PrefetchScalarGridSpec(
            num_scalar_prefetch=1,
            grid=(1,),
            in_specs=[pl.BlockSpec(own.shape, lambda k, order: (0, 0))],
            out_specs=pl.BlockSpec(own.shape, lambda k, order: (order[0], 0)),
        ),
        out_shape=jax.ShapeDtypeStruct((8 * own.shape[0], own.shape[1]), own.dtype),
        compiler_params=ROOMY,
        cost_estimate=QUICK,
        name="placed_own",
    )(member_order(), own)


def gather_rows(own, near):
    count = own.shape[0]
    half = count // 2
    near, whole = lax.optimization_barrier((near, placed_own(own)))
    along_x, along_y = near
    first_half, second_half = swap(along_x[:half], 4), swap(along_y[half:], 2)
    placed = [
        (1, 0, swap(own, 1)),
        (2, 0, along_x),
        (4, 0, along_y),
        (3, 0, swap(along_x, 1)),
        (5, 0, swap(along_y, 1)),
        (6, 0, first_half),
        (6, half, second_half),
        (7, 0, swap(first_half, 1)),
        (7, half, swap(second_half, 1)),
    ]
    for k, offset, block in placed:
        whole = lax.dynamic_update_slice(whole, block, (member_of(k) * count + offset, 0))
    return whole


def gather_plain(own):
    return lax.all_gather(own, "fsdp", axis=0, tiled=True)


def gather_small(own):
    held = own[None]
    for bits in (1, 2, 4):
        held = jnp.concatenate([held, swap(held, bits)], axis=0)
    return relative(held, 0)


def scatter_rows(array):
    return lax.psum_scatter(array, "fsdp", scatter_dimension=0, tiled=True)


def exchange_blocks(blocks):
    if not by_xor():
        moved = lax.all_to_all(jnp.stack(blocks), "fsdp", 0, 0, tiled=True)
        return [moved[k] for k in range(len(blocks))]
    moved = {0: blocks[0]}
    for k in (2, 4, 6, 1, 3, 5, 7):
        moved[k] = swap(blocks[k], k)
    return [moved[k] for k in range(8)]


def relative(array, axis):
    if not by_xor():
        return array
    step = array.shape[axis] // 8
    return jnp.concatenate(
        [lax.dynamic_slice_in_dim(array, member_of(k) * step, step, axis) for k in range(8)],
        axis=axis,
    )


def columns_sent(own):
    planes = lax.axis_size("ctx")
    part, share = own.shape[0] // planes, own.shape[1] // 8
    place = lax.axis_index("ctx")
    return [
        lax.dynamic_slice(own, (place * part, member_of(k) * share), (part, share)) for k in range(8)
    ]


def columns_held(moved):
    held = jnp.zeros((8,) + moved[0].shape, moved[0].dtype)
    for k in range(8):
        held = lax.dynamic_update_slice(held, moved[k][None], (member_of(k), 0, 0))
    return held


def next_plane(held):
    planes = lax.axis_size("ctx")
    return lax.ppermute(held, "ctx", [(i, (i + 1) % planes) for i in range(planes)])


def columns_whole(held_parts):
    planes = len(held_parts)
    peers, part, share = held_parts[0].shape
    whole = jnp.zeros((peers, planes, part, share), held_parts[0].dtype)
    for step, held in enumerate(held_parts):
        source = lax.rem(lax.axis_index("ctx") + planes - step, planes)
        whole = lax.dynamic_update_slice(whole, held[:, None], (0, source, 0, 0))
    return whole.reshape(peers * planes * part, share)


def tick_body(at_end_ref, given, *refs):
    names = [name for name, there in given if there]
    held = dict(zip(names, refs))
    made = list(refs[len(names) :])

    def add(first, second):
        return (held[first][...].astype(FULL) + held[second][...].astype(FULL)).astype(LOW)

    if "fresh" in held:
        made.pop(0)[...] = add("fresh", "from_end")
    if "middle" in held:
        total = add("middle", "other")
        if "later" in held:
            total = jnp.where(at_end_ref[0] == 1, held["later"][...], total)
        made.pop(0)[...] = total


class SumOverCtx:
    def __init__(self, first):
        self.on_line = lax.axis_size("ctx") == 4
        place = lax.axis_index("ctx")
        self.ends = ((place == 0) | (place == 3)).astype(jnp.int32)[None]
        self.state = (first, None, None, first)
        self.results = []
        self.fenced = 0

    def combine(self, **arrays):
        given = {name: array for name, array in arrays.items() if array is not None}
        shape = next(iter(given.values())).shape
        count = ("fresh" in given) + ("middle" in given)
        spec = pl.BlockSpec(memory_space=pltpu.VMEM)
        flags = [(name, name in given) for name in arrays]
        return pl.pallas_call(
            lambda at_end_ref, *refs: tick_body(at_end_ref, flags, *refs),
            in_specs=[pl.BlockSpec(memory_space=pltpu.SMEM)] + [spec] * len(given),
            out_specs=[spec] * count,
            out_shape=[jax.ShapeDtypeStruct(shape, LOW)] * count,
            compiler_params=pltpu.CompilerParams(vmem_limit_bytes=32 * 2**20),
            cost_estimate=QUICK,
            name="tick",
        )(self.ends, *given.values())

    def move(self, later=None):
        fresh, middle, outgoing, incoming = self.state
        if not self.on_line:
            if fresh is not None:
                total = lax.psum(fresh, "ctx")
                self.results.append((total, total))
            self.state = (later, None, None, None)
            return
        inward, outward = [(0, 1), (3, 2)], [(1, 0), (2, 3)]
        from_end = other = None
        if outgoing is not None and outgoing is incoming:
            from_end = from_middle = lax.ppermute(outgoing, "ctx", inward + outward)
        else:
            if fresh is not None:
                from_end = lax.ppermute(incoming, "ctx", inward)
            if outgoing is not None:
                from_middle = lax.ppermute(outgoing, "ctx", outward)
        if outgoing is not None:
            self.results.append((from_middle, outgoing))
        if middle is not None:
            other = lax.ppermute(middle, "ctx", [(1, 2), (2, 1)])
        pair_sum = total = None
        joined = middle is not None and later is not None and later.shape == middle.shape
        alike = fresh is None or middle is None or fresh.shape == middle.shape
        chosen = later if joined else None
        if alike and (fresh is not None or middle is not None):
            made = self.combine(
                fresh=fresh, from_end=from_end, middle=middle, other=other, later=chosen
            )
            pair_sum = made[0] if fresh is not None else None
            total = made[-1] if middle is not None else None
        elif fresh is not None:
            (pair_sum,) = self.combine(fresh=fresh, from_end=from_end)
            (total,) = self.combine(middle=middle, other=other, later=chosen)
        self.state = (later, pair_sum, total, total if joined else later)

    def fence(self, *values):
        fresh, middle, outgoing, incoming = self.state
        joined = outgoing is not None and outgoing is incoming
        held = (fresh, middle, outgoing, None if joined or incoming is fresh else incoming)
        made = self.results[self.fenced :]
        held, made, values = lax.optimization_barrier((held, made, values))
        self.results[self.fenced :] = made
        self.fenced = len(self.results)
        incoming = held[2] if joined else held[0]
        self.state = (held[0], held[1], held[2], incoming)
        return values


def attend_kernel(query_ref, key_ref, value_t_ref, mask_ref, out_ref, total_ref):
    scores = product_nt(key_ref[...], query_ref[...]) * (SCALING * LOG2E) + mask_ref[...]
    largest = jnp.max(scores, axis=0, keepdims=True)
    weights = jnp.exp2(scores - largest)
    weight_sum = jnp.sum(weights, axis=0, keepdims=True)
    gathered = product(value_t_ref[...], weights.astype(LOW))
    out_ref[...] = (gathered / weight_sum).T.astype(LOW)
    total_ref[0] = largest + jnp.log2(weight_sum)


def attend(queries, keys, values_t, mask):
    rows, key_rows = queries.shape[0], keys.shape[0]
    whole = lambda head: (0, 0)
    by_head = lambda head: (0, head)
    return pl.pallas_call(
        attend_kernel,
        grid=(H,),
        in_specs=[
            pl.BlockSpec((rows, HD), by_head),
            pl.BlockSpec((key_rows, HD), whole),
            pl.BlockSpec((HD, key_rows), whole),
            pl.BlockSpec((key_rows, rows), whole),
        ],
        out_specs=[
            pl.BlockSpec((rows, HD), by_head),
            pl.BlockSpec((1, 1, rows), lambda head: (head, 0, 0)),
        ],
        out_shape=[
            jax.ShapeDtypeStruct((rows, H * HD), LOW),
            jax.ShapeDtypeStruct((H, 1, rows), FULL),
        ],
        compiler_params=ROOMY,
        cost_estimate=QUICK,
        name="attend",
    )(queries, keys, values_t, mask)


def attend_back_kernel(
    query_ref,
    grad_ref,
    out_ref,
    total_ref,
    key_ref,
    key_t_ref,
    value_ref,
    mask_ref,
    grad_query_ref,
    grad_key_ref,
    grad_value_ref,
):
    @pl.when(pl.program_id(0) == 0)
    def _():
        grad_key_ref[...] = jnp.zeros_like(grad_key_ref)
        grad_value_ref[...] = jnp.zeros_like(grad_value_ref)

    query, grad = query_ref[...], grad_ref[...]
    scores = product_nt(key_ref[...], query) * (SCALING * LOG2E) + mask_ref[...]
    probs = jnp.exp2(scores - total_ref[0])
    grad_probs = product_nt(value_ref[...], grad)
    delta = jnp.sum((grad.astype(FULL) * out_ref[...].astype(FULL)).T, axis=0, keepdims=True)
    grad_scores = (probs * (grad_probs - delta)).astype(LOW)
    grad_value_ref[...] += product(probs.astype(LOW), grad)
    grad_key_ref[...] += product(grad_scores, query)
    grad_query_ref[...] = (product(key_t_ref[...], grad_scores).T * SCALING).astype(LOW)


def attend_back(queries, grad_out, out, totals, keys, keys_t, values, mask):
    rows, key_rows = queries.shape[0], keys.shape[0]
    whole = lambda head: (0, 0)
    by_head = lambda head: (0, head)
    return pl.pallas_call(
        attend_back_kernel,
        grid=(H,),
        in_specs=[
            pl.BlockSpec((rows, HD), by_head),
            pl.BlockSpec((rows, HD), by_head),
            pl.BlockSpec((rows, HD), by_head),
            pl.BlockSpec((1, 1, rows), lambda head: (head, 0, 0)),
            pl.BlockSpec((key_rows, HD), whole),
            pl.BlockSpec((HD, key_rows), whole),
            pl.BlockSpec((key_rows, HD), whole),
            pl.BlockSpec((key_rows, rows), whole),
        ],
        out_specs=[
            pl.BlockSpec((rows, HD), by_head),
            pl.BlockSpec((key_rows, HD), whole),
            pl.BlockSpec((key_rows, HD), whole),
        ],
        out_shape=[
            jax.ShapeDtypeStruct((rows, H * HD), LOW),
            jax.ShapeDtypeStruct((key_rows, HD), FULL),
            jax.ShapeDtypeStruct((key_rows, HD), FULL),
        ],
        compiler_params=ROOMY,
        cost_estimate=QUICK,
        name="attend_back",
    )(queries, grad_out, out, totals, keys, keys_t, values, mask)


def normalize(values_in):
    center = values_in - jnp.mean(values_in, axis=-1, keepdims=True)
    spread = jnp.mean(center * center, axis=-1, keepdims=True)
    inverse = lax.rsqrt(spread + EPSILON)
    return center * inverse, inverse


def norm_pullback(normed, inverse, gain, grad_in, base, pair=None, weight=None, out_type=FULL):
    rows, width = normed.shape
    more = [] if pair is None else [pair, weight]

    def body(normed_ref, inverse_ref, gain_ref, grad_ref, base_ref, *refs):
        out_ref, sums_ref = refs[-2:]
        grad = grad_ref[...].astype(FULL)
        if more:
            grad = grad + product_nt(refs[0][...], refs[1][...])
        held = normed_ref[...]
        weighted = grad * gain_ref[...]
        turned = inverse_ref[...] * (
            weighted
            - jnp.mean(weighted, axis=-1, keepdims=True)
            - held * jnp.mean(weighted * held, axis=-1, keepdims=True)
        )
        made = base_ref[...].astype(FULL) + turned
        out_ref[...] = made.astype(out_type)
        sums_ref[0:1] = jnp.sum(grad * held, axis=0, keepdims=True)
        sums_ref[1:2] = jnp.sum(grad, axis=0, keepdims=True)
        sums_ref[2:3] = jnp.sum(made.astype(LOW).astype(FULL), axis=0, keepdims=True)

    at = lambda i: (0, 0)
    specs = [pl.BlockSpec(array.shape, at) for array in (normed, inverse, gain[None], grad_in, base)]
    if more:
        cols = pair.shape[1]
        last = weight.shape[1] // cols - 1
        specs += [pl.BlockSpec(pair.shape, at), pl.BlockSpec((width, cols), lambda i: (0, last))]
    made, sums = pl.pallas_call(
        body,
        grid=(1,),
        in_specs=specs,
        out_specs=[pl.BlockSpec((rows, width), at), pl.BlockSpec((8, width), at)],
        out_shape=[
            jax.ShapeDtypeStruct((rows, width), out_type),
            jax.ShapeDtypeStruct((8, width), FULL),
        ],
        compiler_params=ROOMY,
        cost_estimate=QUICK,
        name="norm_pullback",
    )(normed, inverse, gain[None], grad_in, base, *more)
    return made, sums[0], sums[1], sums[2]


def gelu_pair(values_in):
    root = math.sqrt(2.0 / math.pi)
    square = values_in * values_in
    turned = jnp.tanh(root * values_in * (1.0 + 0.044715 * square))
    slope = 0.5 * (1.0 + turned) + 0.5 * values_in * (1.0 - turned * turned) * root * (
        1.0 + 3.0 * 0.044715 * square
    )
    return 0.5 * values_in * (1.0 + turned), slope


def per_device(
    tokens,
    segments,
    query_weight,
    pair_weight,
    out_weight,
    query_bias,
    value_bias,
    out_bias,
    norm1_gain,
    norm1_bias,
    fc_weight,
    proj_weight,
    fc_bias,
    proj_bias,
    norm2_gain,
    norm2_bias,
    cotangent,
):
    rows, width = tokens.shape[1:]
    peers = lax.axis_size("fsdp")
    depth_share = width // peers
    ctx_count = lax.axis_size("ctx")
    ctx_index = lax.axis_index("ctx")
    members = range(peers)

    spelled = by_xor() and ctx_count == 4
    ff_share = fc_weight.shape[1] // peers
    cot_own = cotangent[0]
    vectors = [query_bias, out_bias, norm1_gain, norm1_bias, proj_bias, norm2_gain, norm2_bias]
    vectors_own = jnp.concatenate(vectors + [value_bias])
    attn_weight = jnp.concatenate([query_weight, pair_weight], axis=1)
    attn_all = gather_plain(attn_weight)
    if spelled:
        packed = gather_small(vectors_own)
        held = columns_held(exchange_blocks(columns_sent(fc_weight)))
        packed, held = lax.optimization_barrier((packed, held))
        held_parts = [held, next_plane(held)]
        attn_all, packed, held_parts, out_sent = lax.optimization_barrier(
            (attn_all, packed, held_parts, out_weight)
        )
        out_near = near_rows(out_sent)
        cot_all = gather_plain(tie(cot_own, attn_all))
    else:
        packed = lax.all_gather(vectors_own, "fsdp", axis=0)
        out_all = gather_plain(out_weight)
        cot_all = gather_plain(cot_own)
        fc_all = lax.all_to_all(fc_weight, "fsdp", 1, 0, tiled=True)
    small = [
        packed[:, i * depth_share : (i + 1) * depth_share].reshape(-1).astype(FULL)
        for i in range(len(vectors))
    ]
    query_bias_all, out_bias_all, gain1, bias1, proj_bias_all, gain2, bias2 = small
    value_bias_all = packed[:, len(vectors) * depth_share :].reshape(-1).astype(FULL)

    tok_rows = tokens[0].astype(FULL)
    normed1, inverse1 = normalize(tok_rows)
    normed_in = (normed1 * gain1 + bias1).astype(LOW)
    attn_bias = jnp.concatenate([query_bias_all, jnp.zeros((HD,), FULL), value_bias_all])
    projected = (product(normed_in, attn_all) + attn_bias).astype(LOW)
    pair_own = projected[:, width:]
    reach = min(ctx_count - 1, -(-(WINDOW - 1) // rows))
    pairs = [pair_own] + [
        lax.ppermute(pair_own, "ctx", [(i, i + d) for i in range(ctx_count - d)])
        for d in range(1, reach + 1)
    ]
    if spelled:
        held_parts, pairs, out_near = lax.optimization_barrier((held_parts, pairs, out_near))
        held_parts = held_parts + [next_plane(held_parts[-1])]
        out_all = gather_rows(out_sent, out_near)
    pair_rows = jnp.concatenate(pairs, axis=0)
    seg_row = segments[0]
    query_first = ctx_index * rows
    key_pos = jnp.concatenate(
        [query_first - d * rows + jnp.arange(rows, dtype=jnp.int32) for d in range(reach + 1)]
    )
    query_pos = query_first + jnp.arange(rows, dtype=jnp.int32)
    query_seg = lax.dynamic_slice_in_dim(seg_row, query_first, rows, 0)
    key_seg = jnp.concatenate(
        [
            lax.dynamic_slice_in_dim(seg_row, jnp.maximum(query_first - d * rows, 0), rows, 0)
            for d in range(reach + 1)
        ]
    )
    allowed = (
        (key_seg[:, None] == query_seg[None, :])
        & (key_pos[:, None] <= query_pos[None, :])
        & (query_pos[None, :] - key_pos[:, None] < WINDOW)
        & (key_pos[:, None] >= 0)
    )
    mask = jnp.where(allowed, 0.0, NEGATIVE).astype(FULL)
    keys, values = pair_rows[:, :HD], pair_rows[:, HD:]
    attended, score_totals = attend(projected, keys, values.T, mask)
    middle = tok_rows + (product(attended, out_all) + out_bias_all)
    normed2, inverse2 = normalize(middle)
    normed_mid = (normed2 * gain2 + bias2).astype(LOW)

    if spelled:
        held_parts, normed_mid = lax.optimization_barrier((held_parts, normed_mid))
        held_parts = held_parts + [next_plane(held_parts[-1])]
        fc_all = columns_whole(held_parts)
        mid_all = gather_rows(normed_mid, near_rows(normed_mid))
    else:
        mid_all = gather_plain(normed_mid)
    fc_bias_own = fc_bias.astype(FULL)
    piece = ff_share // 4
    ff_args = (mid_all, fc_all, fc_bias_own, cot_all, proj_weight)
    hidden, grad_pre = feed_forward(*ff_args, 0)

    def proj_term(j):
        return matmul(hidden, cot_all, "tn", 256, 1024, j * piece, piece)

    sums = SumOverCtx(proj_term(0))
    ff_args, hidden, grad_pre = sums.fence(ff_args, hidden, grad_pre)

    mid_all, fc_all, unused, cot_all, unused = ff_args
    later = proj_term(1)
    hidden, grad_pre = feed_forward(*ff_args, 1, (hidden, grad_pre))
    sums.move(later)
    mid_all, fc_all, cot_all, hidden, grad_pre = sums.fence(
        mid_all, fc_all, cot_all, hidden, grad_pre
    )

    grad_mid_part = matmul(grad_pre, fc_all, "nt")
    grad_normed_mid = scatter_rows(grad_mid_part)
    fc_terms = fc_gradient(mid_all, grad_pre)
    sums.move(proj_term(2))
    cot_all, hidden, grad_pre, grad_mid_part, fc_terms = sums.fence(
        cot_all, hidden, grad_pre, grad_mid_part, fc_terms
    )

    share_half, group = depth_share // 2, peers // 2
    fc_first = exchange_blocks([fc_terms[k, :share_half] for k in members])
    grad_fc_bias = jnp.sum(grad_pre.astype(FULL), axis=0)
    cot_sum = jnp.sum(cot_own.astype(FULL), axis=0)
    sums.move(proj_term(3))
    hidden, fc_terms, fc_first, grad_fc_bias, cot_sum = sums.fence(
        hidden, fc_terms, fc_first, grad_fc_bias, cot_sum
    )

    fc_second = exchange_blocks([fc_terms[k, share_half:] for k in members])
    sums.move(jnp.concatenate(fc_first[:group], axis=1))
    fc_first, fc_second, grad_normed_mid = sums.fence(fc_first, fc_second, grad_normed_mid)

    grad_middle, grad_gain2, grad_bias2, grad_mid_sum = norm_pullback(
        normed2, inverse2, gain2, grad_normed_mid, cot_own
    )
    grad_mid_low = grad_middle.astype(LOW)
    grad_attended = matmul(grad_mid_low, out_all, "nt", 256, 512)
    out_term = matmul(attended, grad_mid_low, "tn", 512, 2048)
    sums.move(jnp.concatenate(fc_first[group:], axis=1))
    fc_second, grad_middle, grad_attended, out_term, grad_mid_sum = sums.fence(
        fc_second, grad_middle, grad_attended, out_term, grad_mid_sum
    )

    out_share = scatter_rows(out_term)
    grad_query_low, grad_keys, grad_values = attend_back(
        projected, grad_attended, attended, score_totals, keys, keys.T, values, mask
    )
    sums.move(jnp.concatenate(fc_second[:group], axis=1))
    fc_second, grad_query_low, grad_keys, grad_values = sums.fence(
        fc_second, grad_query_low, grad_keys, grad_values
    )

    grad_pairs = jnp.concatenate([grad_keys, grad_values], axis=1)
    grad_pair = grad_pairs[:rows]
    for d in range(1, reach + 1):
        sent = grad_pairs[d * rows : (d + 1) * rows].astype(LOW)
        grad_pair = grad_pair + lax.ppermute(
            sent, "ctx", [(i + d, i) for i in range(ctx_count - d)]
        ).astype(FULL)
    pair_scaling = jnp.concatenate([jnp.full((HD,), SCALING, FULL), jnp.ones((HD,), FULL)])
    grad_pair_low = (grad_pair * pair_scaling).astype(LOW)
    grad_normed_in = matmul(grad_query_low, attn_all, "nt", 256, 512, out_type=FULL)
    query_sum = jnp.sum(grad_query_low.astype(FULL), axis=0)
    fc_second, grad_query_low, grad_pair_low, grad_normed_in, query_sum = sums.fence(
        fc_second, grad_query_low, grad_pair_low, grad_normed_in, query_sum
    )

    grad_tokens, grad_gain1, grad_bias1, unused = norm_pullback(
        normed1,
        inverse1,
        gain1,
        grad_normed_in,
        grad_middle,
        grad_pair_low,
        attn_all,
        LOW,
    )
    pair_sum = jnp.sum(grad_pair_low.astype(FULL), axis=0)
    vector_terms = [
        query_sum,
        grad_mid_sum,
        grad_gain1,
        grad_bias1,
        cot_sum,
        grad_gain2,
        grad_bias2,
    ]
    by_member = jnp.concatenate(
        [term.reshape(peers, depth_share) for term in vector_terms]
        + [pair_sum[HD:].reshape(peers, HD // peers)],
        axis=1,
    )
    used, extra_cols = by_member.shape[1], attn_all.shape[1]
    by_member = jnp.pad(by_member, ((0, 0), (0, extra_cols - used)))
    grad_fc_bias = jnp.pad(grad_fc_bias, (0, extra_cols - ff_share))
    is_own = jnp.arange(peers)[:, None] == lax.axis_index("fsdp")
    fc_bias_rows = jnp.where(is_own, grad_fc_bias[None], 0.0)
    extra = jnp.stack([by_member, fc_bias_rows], axis=1).astype(LOW)
    extra = jnp.pad(extra, ((0, 0), (0, 14), (0, 0)))
    attn_term = attn_gradient(normed_in, grad_query_low, grad_pair_low, extra)
    attn_rows = attn_term.shape[1]
    attn_term = attn_term.reshape(peers * attn_rows, extra_cols)
    attn_share = scatter_rows(attn_term)
    sums.move(jnp.concatenate(fc_second[group:], axis=1))
    hidden, attn_term = sums.fence(hidden, attn_term)

    out_part = matmul(hidden, proj_weight, "nn")
    sums.move(out_share)
    (out_part,) = sums.fence(out_part)

    grad_proj = finish(sums.ends, sums.results[:4], 1)
    attn_cut = (attn_rows + 16) // 32 * 16
    sums.move(attn_share[:attn_cut])
    grad_proj, out_part = sums.fence(grad_proj, out_part)

    out_sum = scatter_rows(out_part).astype(FULL)
    output = (middle + (out_sum + proj_bias_all)).astype(LOW)
    sums.move(attn_share[attn_cut:])
    sums.fence()
    if spelled:
        grad_fc = finish(sums.ends, sums.results[4:8], 2, group)
    sums.move()
    sums.fence()
    sums.move()
    sums.fence()
    sums.move()
    sums.fence()
    if not spelled:
        grad_fc = finish(sums.ends, sums.results[4:8], 2, group)
    grad_out, attn_first, attn_second = [
        jnp.where(sums.ends[0] == 1, at_end, inside).astype(FULL)
        for at_end, inside in sums.results[8:]
    ]
    attn_sums = jnp.concatenate([attn_first, attn_second], axis=0)
    vector_sum, grad_fc_bias = attn_sums[depth_share], attn_sums[depth_share + 1, :ff_share]
    shares = [vector_sum[i * depth_share : (i + 1) * depth_share] for i in range(len(vectors))]
    value_share = vector_sum[len(vectors) * depth_share : used]
    return (
        output[None],
        grad_tokens[None],
        attn_sums[:depth_share, :width],
        attn_sums[:depth_share, width:],
        grad_out,
        shares[0],
        value_share,
        shares[1],
        shares[2],
        shares[3],
        grad_fc,
        grad_proj,
        grad_fc_bias,
        shares[4],
        shares[5],
        shares[6],
    )


def solution(mesh):
    weight, vector, token = P("fsdp", None), P("fsdp"), P("fsdp", "ctx", None)
    return jax.shard_map(
        per_device,
        mesh=mesh,
        in_specs=(
            token,
            weight,
            weight,
            weight,
            weight,
            vector,
            vector,
            vector,
            vector,
            vector,
            weight,
            weight,
            vector,
            vector,
            vector,
            vector,
            token,
        ),
        out_specs=(
            token,
            token,
            weight,
            weight,
            weight,
            vector,
            vector,
            vector,
            vector,
            vector,
            weight,
            weight,
            vector,
            vector,
            vector,
            vector,
        ),
        check_vma=False,
    )
```
